32 devices in a mesh: modes: 8 (over y, x, core), sub: 4 (over z).
Axes of the slice: x: 2, y: 2, z: 4, core: 2. Of those that a mesh axis runs over, the one named last changes fastest.
Arguments:
- fields: bfloat16 [2, 384, 1024, 512], P(None, 'sub', 'modes'), may hold values from -6 to 6
- previous: float32 [384, 128, 2, 512], P('sub', 'modes'), may hold values from -6 to 6
- eigen_vectors: float32 [4, 96, 96], P('sub'), may hold values from -0.625 to 0.625
- eigen_map: float32 [4, 96, 96], P('sub'), may hold values from -0.625 to 0.625
- eigen_magnitude: float32 [384], P('sub'), may hold values from 0.5 to 20
- end_rows: float32 [4, 2, 96], P('sub'), may hold values from -0.625 to 0.625
Outputs:
- potential: float32 [384, 128, 2, 512], P('sub', 'modes')
The draws below stay inside these ranges and needn't reach their ends.
All inputs are finite; a program needn't handle non-finite values.
Results may differ from the reference program's by a relative error of at most 0.0032.
Values may be sent and summed in bfloat16 or wider, within the bound.
No kernel may reach another device: no remote copies, remote signals or barrier semaphores. Data moves between devices by JAX's collectives and lax.ppermute only.
A program may use at most 128 MiB of HBM per device.

```python
import math
import jax
import jax.numpy as jnp
from jax import lax

CHEB = 96
NXP = 1024
NZP = 512
KZ = 128
KX = 512
YTOT = 384
N_SUB = 4


def steps_of(own_key, dims, pieces, low, top_value):
    factor_of, own = 1.0, jax.random.fold_in(own_key, 6)
    for axis_at, parts in pieces:
        steps = jnp.exp(jax.random.uniform(jax.random.fold_in(own, axis_at), (parts,), jnp.float32, low / len(pieces), top_value / len(pieces)))
        factor_of = factor_of * jnp.repeat(steps, dims[axis_at] // parts).reshape([-1 if axis == axis_at else 1 for axis in range(len(dims))])
    return factor_of


def gaussian(key, dims, width, limit, split=(), held_as=jnp.bfloat16):
    result = width * jax.random.normal(key, dims, jnp.float32)
    if split:
        result = result * steps_of(key, dims, split, -0.22, 0.18)
    return jnp.clip(result, -limit, limit).astype(held_as)


def setup_inputs(seed: int = 0) -> dict:
    arg_keys = jax.random.split(jax.random.key(seed), 7)
    return {
        "fields": gaussian(arg_keys[0], (2, YTOT, NXP, NZP), 1.0, 6.0, ((1, 4), (2, 8))),
        "previous": gaussian(arg_keys[1], (YTOT, KZ, 2, KX), 1.0, 6.0, ((0, 4), (1, 8)), jnp.float32),
        "eigen_vectors": gaussian(arg_keys[2], (N_SUB, CHEB, CHEB), CHEB ** -0.5, 0.625, ((0, 4),), jnp.float32),
        "eigen_map": gaussian(arg_keys[3], (N_SUB, CHEB, CHEB), CHEB ** -0.5, 0.625, ((0, 4),), jnp.float32),
        "eigen_magnitude": jnp.clip(jnp.exp(math.log(20.0) - 3.6888795 * jax.random.uniform(arg_keys[4], (YTOT,), jnp.float32) ** steps_of(arg_keys[4], (YTOT,), ((0, 4),), -0.2, 0.2)), 0.5, 20.0),
        "end_rows": gaussian(arg_keys[5], (N_SUB, 2, CHEB), CHEB ** -0.5, 0.625, ((0, 4),), jnp.float32),
    }


TWO_PI = 2.0 * math.pi
WAVE_SCALE = 0.0007
SHIFT_TERM = 0.06

def rounded(values):
    return lax.optimization_barrier(values.astype(jnp.bfloat16)).astype(jnp.float32)

def spanwise_table(wave_index, points):
    grid = jnp.arange(points, dtype=jnp.int32)
    phase = grid[:, None] * wave_index[None, :] % points
    angle = TWO_PI / points * phase.astype(jnp.float32)
    scale = 1.0 / math.sqrt(points)
    return (jnp.stack([jnp.cos(angle), -jnp.sin(angle)], axis=1) * scale).astype(jnp.bfloat16)

def streamwise_table(points, count):
    grid = jnp.arange(points, dtype=jnp.int32)
    waves = jnp.arange(count, dtype=jnp.int32) - count // 2
    phase = grid[:, None] * waves[None, :] % points
    angle = TWO_PI / points * phase.astype(jnp.float32)
    cosine = jnp.cos(angle)
    sine = jnp.sin(angle)
    scale = 1.0 / math.sqrt(points)
    real_row = jnp.concatenate([cosine, -sine], axis=1)
    imag_row = jnp.concatenate([sine, cosine], axis=1)
    return (jnp.stack([real_row, imag_row], axis=1) * scale).astype(jnp.bfloat16)

def wall_terms(kappa, cheb):
    points = jnp.cos(math.pi * (jnp.arange(cheb, dtype=jnp.float32) + 1.0) / (cheb + 1))
    points = points[:, None, None, None]
    rate = kappa[None, :, None, :]
    divisor = 1.0 - jnp.exp(-4.0 * rate)
    lower = jnp.exp(-rate * (1.0 + points)) * (1.0 - jnp.exp(-2.0 * rate * (1.0 - points))) / divisor
    upper = jnp.exp(-rate * (1.0 - points)) * (1.0 - jnp.exp(-2.0 * rate * (1.0 + points))) / divisor
    return (lower, upper)

def reference(fields, previous, eigen_vectors, eigen_map, eigen_magnitude, end_rows):
    high = lax.Precision.HIGHEST
    table_z = rounded(spanwise_table(jnp.arange(KZ, dtype=jnp.int32), NZP))
    table_x = rounded(streamwise_table(NXP, KX))
    waves_x = jnp.arange(KX, dtype=jnp.float32) - float(KX // 2)
    waves_z = jnp.arange(KZ, dtype=jnp.float32)
    kappa_sq = SHIFT_TERM + (WAVE_SCALE * waves_x[None, :]) ** 2 + (WAVE_SCALE * waves_z[:, None]) ** 2
    kappa = jnp.sqrt(kappa_sq)
    decay_four = jnp.exp(-4.0 * kappa)
    coth_term = ((1.0 + decay_four) / (1.0 - decay_four))[:, None, :]
    csch_term = (2.0 * jnp.exp(-2.0 * kappa) / (1.0 - decay_four))[:, None, :]
    freq_x = TWO_PI * waves_x / NXP
    particulars = []
    trace_list = []
    for index in range(N_SUB):
        start = index * CHEB
        stop = start + CHEB
        stress = rounded(fields[0, start:stop].astype(jnp.float32) * fields[1, start:stop].astype(jnp.float32))
        half_spectrum = rounded(jnp.einsum('cxz,zrk->cxrk', stress, table_z, precision=high))
        stress_hat = jnp.einsum('cxrk,xrq->ckq', half_spectrum, table_x, precision=high)
        stress_hat = stress_hat.reshape(CHEB, KZ, 2, KX)
        prior = previous[start:stop]
        forcing_re = prior[:, :, 0] + freq_x * stress_hat[:, :, 1]
        forcing_im = prior[:, :, 1] - freq_x * stress_hat[:, :, 0]
        forcing = jnp.stack([forcing_re, forcing_im], axis=2)
        coefficients = jnp.einsum('ij,jkrq->ikrq', eigen_map[index], forcing, precision=high)
        coefficients = coefficients / -(eigen_magnitude[start:stop][:, None, None, None] + kappa_sq[None, :, None, :])
        particular = jnp.einsum('ij,jkrq->ikrq', eigen_vectors[index], coefficients, precision=high)
        traces = jnp.einsum('ej,jkrq->ekrq', end_rows[index], particular, precision=high)
        particulars.append(particular)
        trace_list.append(traces)
    c_prev = jnp.zeros((KZ, 1, KX), jnp.float32)
    d_prev = jnp.zeros((KZ, 2, KX), jnp.float32)
    c_list = []
    d_list = []
    for index in range(1, N_SUB):
        jump_value = (trace_list[index][0] - trace_list[index - 1][1]) / kappa[:, None, :]
        divisor = 2.0 * coth_term - -csch_term * c_prev
        c_prev = -csch_term / divisor
        d_prev = (jump_value - -csch_term * d_prev) / divisor
        c_list.append(c_prev)
        d_list.append(d_prev)
    solved = [None] * (N_SUB - 1)
    g_next = jnp.zeros((KZ, 2, KX), jnp.float32)
    for index in range(N_SUB - 2, -1, -1):
        g_next = d_list[index] - c_list[index] * g_next
        solved[index] = g_next
    zero_value = jnp.zeros((KZ, 2, KX), jnp.float32)
    padded = [zero_value] + solved + [zero_value]
    lower, upper = wall_terms(kappa, CHEB)
    outputs = []
    for index in range(N_SUB):
        outputs.append(particulars[index] + padded[index][None] * lower + padded[index + 1][None] * upper)
    return jnp.concatenate(outputs, axis=0)
```

```python
import functools
import math

import jax
import jax.numpy as jnp
import ml_dtypes
import numpy as np
from jax import lax
from jax.experimental import pallas as pl
from jax.experimental.pallas import tpu as pltpu
from jax.sharding import PartitionSpec as P

TWO_PI = 2.0 * math.pi
WAVE_SCALE = 0.0007
SHIFT_TERM = 0.06
CHUNK = 4
GROUP = 2 * CHUNK
LANES = 128
BF16 = jnp.bfloat16
F32 = jnp.float32
VMEM_LIMIT = 57 * 1024 * 1024
TILE = 256
AFTER = 4
SHARES = (3, 1)
JOINED = (False, True)
HEAD_JOINED = True
BODY_BLOCK = 16
HEAD_ROWS = 32


def spanwise_rows(points, modes_count, kz_local):
    grid = np.arange(points)
    waves = np.arange(modes_count * kz_local)
    angle = TWO_PI / points * ((grid[None, :] * waves[:, None]) % points)
    both = np.stack([np.cos(angle), -np.sin(angle)], axis=0) / math.sqrt(points)
    both = both.reshape(2, modes_count, kz_local // CHUNK, CHUNK, points)
    both = both.transpose(1, 2, 0, 3, 4).reshape(modes_count, 2 * kz_local, points)
    return both.astype(np.float32).astype(ml_dtypes.bfloat16)


def streamwise_rows(points, modes_count, count):
    grid = np.arange(points)
    waves = np.arange(count) - count // 2
    angle = TWO_PI / points * ((grid[:, None] * waves[None, :]) % points)
    both = np.concatenate([np.cos(angle), np.sin(angle)], axis=1) / math.sqrt(points)
    both = both.reshape(modes_count, points // modes_count, 2 * count)
    return both.astype(np.float32).astype(ml_dtypes.bfloat16)


def split_pair(value):
    high = value.astype(BF16)
    low = (value - high.astype(F32)).astype(BF16)
    return high, low


def paired_map(matrix):
    high, low = split_pair(matrix)
    return jnp.concatenate(
        [jnp.concatenate([high, high], axis=1), jnp.concatenate([low, low], axis=1)], axis=0
    )


def full_spec():
    return pl.BlockSpec(memory_space=pltpu.VMEM)


def scalar_spec():
    return pl.BlockSpec(memory_space=pltpu.SMEM)


def params(limit=VMEM_LIMIT):
    return pltpu.CompilerParams(vmem_limit_bytes=limit)


def span_kernel(modes_count, sets, block, where, fields, table, *rest):
    outs, rows = rest[:-1], rest[-1]
    per_dest = table.shape[1]
    points = table.shape[2]
    me = where[0]

    @pl.when(pl.program_id(0) == 0)
    def _():
        for step in range(modes_count):
            rows[step * per_dest : (step + 1) * per_dest, :] = table[me ^ step]

    x_local = fields.shape[2]
    for pair in range(block // 2):
        stress = fields[0, 2 * pair : 2 * pair + 2] * fields[1, 2 * pair : 2 * pair + 2]
        stress = stress.reshape(2 * x_local, points)
        spectrum = lax.dot_general(
            rows[...], stress, (((1,), (1,)), ((), ())), preferred_element_type=F32
        )
        span = slice(2 * GROUP * pair, 2 * GROUP * (pair + 1))
        for step in range(modes_count):
            at = 0
            for joined, group in sets:
                for place, chunk in enumerate(group):
                    start = step * per_dest + chunk * GROUP
                    piece = spectrum[start : start + GROUP]
                    piece = jnp.concatenate([piece[:, :x_local], piece[:, x_local:]], axis=0)
                    if joined:
                        outs[at][me ^ step, place, span, :] = piece.astype(BF16)
                    else:
                        outs[at + step][place, span, :] = piece.astype(BF16)
                at += 1 if joined else modes_count


def span_part(fields, table, where, first, count, sets, block):
    modes_count, per_dest, points = table.shape
    x_local = fields.shape[2]
    shapes, specs = [], []
    for joined, group in sets:
        if joined:
            head = (modes_count, len(group))
            shapes.append(jax.ShapeDtypeStruct(head + (count * GROUP, x_local), BF16))
            specs.append(pl.BlockSpec(head + (block * GROUP, x_local), lambda i, w: (0, 0, i, 0)))
            continue
        for _ in range(modes_count):
            shapes.append(jax.ShapeDtypeStruct((len(group), count * GROUP, x_local), BF16))
            specs.append(
                pl.BlockSpec((len(group), block * GROUP, x_local), lambda i, w: (0, i, 0))
            )
    outs = pl.pallas_call(
        functools.partial(span_kernel, modes_count, sets, block),
        out_shape=shapes,
        grid_spec=pltpu.PrefetchScalarGridSpec(
            num_scalar_prefetch=1,
            grid=(count // block,),
            in_specs=[
                pl.BlockSpec((2, block, x_local, points), lambda i, w: (0, first // block + i, 0, 0)),
                pl.BlockSpec(table.shape, lambda i, w: (0, 0, 0)),
            ],
            out_specs=specs,
            scratch_shapes=[pltpu.VMEM((modes_count * per_dest, points), BF16)],
        ),
        compiler_params=params(),
        cost_estimate=pl.CostEstimate(
            flops=2 * count * x_local * points * modes_count * per_dest,
            bytes_accessed=count * x_local * points * 5,
            transcendentals=0,
        ),
        name="span",
    )(where, fields, table)
    result, at = [], 0
    for joined, group in sets:
        if joined:
            result.append(outs[at])
            at += 1
        else:
            result.append(outs[at : at + modes_count])
            at += modes_count
    return result


def kappa_rows(first, rows, count, span):
    waves_x = lax.broadcasted_iota(jnp.int32, (rows, count), 1) - count // 2
    waves_z = lax.broadcasted_iota(jnp.int32, (rows, count), 0) // span + first
    scaled_x = WAVE_SCALE * waves_x.astype(F32)
    scaled_z = WAVE_SCALE * waves_z.astype(F32)
    return SHIFT_TERM + scaled_x * scaled_x + scaled_z * scaled_z


def stream_kernel(modes_count, parts, first, kz_local, where, prev, tables, m_ref, v_ref, e_ref, lam, *rest):
    sources, rest = rest[: sum(n for n, _ in parts)], rest[sum(n for n, _ in parts) :]
    particular, traces_out, forcing = rest
    cheb = m_ref.shape[0]
    count = tables.shape[2] // 2
    points = modes_count * tables.shape[1]
    me = where[0]
    blocks = count // LANES
    place = pl.program_id(0)
    step = pl.program_id(1)

    waves = (lax.broadcasted_iota(jnp.int32, (1, count), 1) - count // 2).astype(F32)
    weight = TWO_PI * waves / points
    row_in = lax.broadcasted_iota(jnp.int32, (GROUP, count), 0)
    signed = jnp.where(row_in < CHUNK, weight, -weight)

    def transform(refs):
        if len(refs) == 1:
            left = [refs[0][d, 0] for d in range(modes_count)]
            origin = list(range(modes_count))
        else:
            left = [ref[0] for ref in refs]
            origin = [me ^ s for s in range(modes_count)]
        left = jnp.concatenate(left, axis=1)
        cosine, sine = [
            jnp.dot(
                left,
                jnp.concatenate([tables[d, :, h * count : (h + 1) * count] for d in origin], axis=0),
                preferred_element_type=F32,
            ).reshape(TILE // GROUP, GROUP, count)
            for h in range(2)
        ]
        cosine = pltpu.roll(cosine, CHUNK, 1)
        total = signed[None] * cosine - weight[None] * sine
        total = total.reshape(TILE, count)
        span = pl.ds(pl.multiple_of(step * TILE, TILE), TILE)
        for b in range(blocks):
            forcing[b, span, :] = total[:, b * LANES : (b + 1) * LANES]

    begin, at = 0, 0
    for arrays, size in parts:
        refs = sources[at : at + arrays]
        pl.when((step >= begin) & (step < begin + size))(functools.partial(transform, refs))
        begin += size
        at += arrays

    @pl.when(step == begin - 1)
    def _():
        map_pair = paired_map(m_ref[...])
        vector_pair = paired_map(v_ref[...])
        end_map = jnp.dot(
            e_ref[...], v_ref[...], preferred_element_type=F32, precision=lax.Precision.HIGHEST
        )
        end_pair = paired_map(end_map)
        magnitude = lam[...]
        width = CHUNK * blocks * 2
        flat = prev.reshape(cheb * width, LANES)
        for k in range(CHUNK):
            sides = []
            for r in range(2):
                for b in range(blocks):
                    new = forcing[b, pl.ds(r * CHUNK + k, cheb, stride=GROUP), :]
                    old = flat[pl.ds((k * blocks + b) * 2 + r, cheb, stride=width), :]
                    sides.append(new + old)
            side = jnp.concatenate(sides, axis=1)
            mapped = jnp.dot(
                map_pair, jnp.concatenate(split_pair(side), axis=0), preferred_element_type=F32
            )
            mapped = mapped[:cheb] + mapped[cheb:]
            kappa_sq = kappa_rows(me * kz_local + (first + place) * CHUNK + k, 1, count, 1)
            inverse = -1.0 / (magnitude + kappa_sq)
            coefficients = mapped * jnp.concatenate([inverse, inverse], axis=1)
            pair = jnp.concatenate(split_pair(coefficients), axis=0)
            value = jnp.dot(vector_pair, pair, preferred_element_type=F32)
            particular[k] = value[:cheb] + value[cheb:]
            ends = jnp.dot(end_pair, pair, preferred_element_type=F32)
            ends = ends[:8] + ends[8:]
            for r in range(2):
                for e in range(2):
                    row = 2 * k + r
                    traces_out[e, row : row + 1, :] = ends[e : e + 1, r * count : (r + 1) * count]


def stream_group(where, prev, tables, m_map, v_map, ends, lam, first, size, sources, offsets, kz_local):
    modes_count = tables.shape[0]
    cheb = m_map.shape[0]
    count = tables.shape[2] // 2
    x_local = tables.shape[1]
    specs, flat, parts, begin = [], [], [], 0
    for source, offset in zip(sources, offsets):
        joined = not isinstance(source, (list, tuple))
        arrays = [source] if joined else list(source)
        held = arrays[0].shape[-2] // TILE

        def index(i, t, w, held=held, offset=offset, begin=begin, head=(0,) * joined):
            return head + (offset + i, jnp.clip(t - begin, 0, held - 1), 0)

        specs += [pl.BlockSpec((modes_count,) * joined + (1, TILE, x_local), index)] * len(arrays)
        flat += arrays
        parts.append((len(arrays), held))
        begin += held
    width = CHUNK * 2 * count // LANES
    flops = 2 * size * begin * TILE * modes_count * x_local * 2 * count

    def whole(array):
        return pl.BlockSpec(array.shape, lambda i, t, w: (0,) * array.ndim)

    return pl.pallas_call(
        functools.partial(stream_kernel, modes_count, parts, first, kz_local),
        out_shape=[
            jax.ShapeDtypeStruct((size * CHUNK, cheb, 2 * count), F32),
            jax.ShapeDtypeStruct((2, size * GROUP, count), F32),
        ],
        grid_spec=pltpu.PrefetchScalarGridSpec(
            num_scalar_prefetch=1,
            grid=(size, begin),
            in_specs=[pl.BlockSpec((cheb, width, LANES), lambda i, t, w: (0, first + i, 0)), full_spec()]
            + [whole(array) for array in (m_map, v_map, ends, lam)]
            + specs,
            out_specs=[
                pl.BlockSpec((CHUNK, cheb, 2 * count), lambda i, t, w: (i, 0, 0)),
                pl.BlockSpec((2, GROUP, count), lambda i, t, w: (0, i, 0)),
            ],
            scratch_shapes=[pltpu.VMEM((count // LANES, begin * TILE, LANES), F32)],
        ),
        compiler_params=params(),
        cost_estimate=pl.CostEstimate(flops=2 * flops, bytes_accessed=4 << 20, transcendentals=0),
        name="stream",
    )(where, prev, tables, m_map, v_map, ends, lam, *flat)


def wall_kernel(kz_local, where, lower_out, upper_out):
    cheb, count = lower_out.shape[1:]
    order = lax.broadcasted_iota(jnp.int32, (cheb, 1), 0).astype(F32)
    points = jnp.cos(math.pi * (order + 1.0) / (cheb + 1))
    chunk = pl.program_id(0)
    for k in range(CHUNK):
        kappa = jnp.sqrt(kappa_rows(where[0] * kz_local + chunk * CHUNK + k, 1, count, 1))
        inverse = 1.0 / (1.0 - jnp.exp(-4.0 * kappa))
        fall = jnp.exp(-kappa * (1.0 + points))
        rise = jnp.exp(-kappa * (1.0 - points))
        lower_out[k] = fall * (1.0 - rise * rise) * inverse
        upper_out[k] = rise * (1.0 - fall * fall) * inverse


def wall_shapes(where, cheb, kz_local, count):
    shape = jax.ShapeDtypeStruct((kz_local, cheb, count), F32)
    return pl.pallas_call(
        functools.partial(wall_kernel, kz_local),
        out_shape=[shape, shape],
        grid=(kz_local // CHUNK,),
        in_specs=[scalar_spec()],
        out_specs=[pl.BlockSpec((CHUNK, cheb, count), lambda i: (i, 0, 0))] * 2,
        compiler_params=params(),
        cost_estimate=pl.CostEstimate(flops=1 << 24, bytes_accessed=6 << 20, transcendentals=2 << 20),
        name="wall",
    )(where)


def finish_kernel(first, kz_local, n_sub, has_old, where, particular, lower, upper, *rest):
    traces = rest[:n_sub]
    out, ordered, solved = rest[n_sub + has_old :]
    cheb = particular.shape[1]
    count = lower.shape[2]
    rows = traces[0].shape[1]
    me = where[1]

    @pl.when(pl.program_id(0) == 0)
    def _():
        for shift in range(n_sub):
            owner = lax.rem(me + n_sub - shift, n_sub)
            ordered[owner] = traces[shift][...]
        kappa = jnp.sqrt(kappa_rows(where[0] * kz_local + first * CHUNK, rows, count, 2))
        decay = jnp.exp(-4.0 * kappa)
        coth_term = (1.0 + decay) / (1.0 - decay)
        csch_term = 2.0 * jnp.exp(-2.0 * kappa) / (1.0 - decay)
        zero = jnp.zeros((rows, count), F32)
        c_prev, d_prev = zero, zero
        factors = []
        for index in range(1, n_sub):
            jump = (ordered[index, 0] - ordered[index - 1, 1]) / kappa
            inverse = 1.0 / (2.0 * coth_term + csch_term * c_prev)
            c_prev = -csch_term * inverse
            d_prev = (jump + csch_term * d_prev) * inverse
            factors.append((c_prev, d_prev))
        solved[0] = zero
        solved[n_sub] = zero
        g_next = zero
        for index in range(n_sub - 1, 0, -1):
            c_value, d_value = factors[index - 1]
            g_next = d_value - c_value * g_next
            solved[index] = g_next

    blocks = count // LANES
    width = CHUNK * 2 * blocks
    flat = out.reshape(cheb * width, LANES)
    chunk = pl.program_id(0)
    for k in range(CHUNK):
        wave = chunk * CHUNK + k
        for r in range(2):
            row = 2 * wave + r
            g_lower = solved[me, pl.ds(row, 1), :]
            g_upper = solved[me + 1, pl.ds(row, 1), :]
            value = (
                particular[k, :, r * count : (r + 1) * count]
                + g_lower * lower[k]
                + g_upper * upper[k]
            )
            for b in range(blocks):
                start = (k * blocks + b) * 2 + r
                flat[pl.ds(start, cheb, stride=width), :] = value[:, b * LANES : (b + 1) * LANES]


def finish_group(where, particular, lower, upper, traces, old, first, kz_local):
    n_sub = len(traces)
    waves, cheb = particular.shape[:2]
    count = lower.shape[2]
    width = CHUNK * 2 * count // LANES
    total = (cheb, kz_local * 2 * count // LANES, LANES)
    has_old = 0 if old is None else 1
    extra = [] if old is None else [old]
    return pl.pallas_call(
        functools.partial(finish_kernel, first, kz_local, n_sub, has_old),
        out_shape=jax.ShapeDtypeStruct(total, F32),
        grid=(waves // CHUNK,),
        in_specs=[
            scalar_spec(),
            pl.BlockSpec((CHUNK, cheb, 2 * count), lambda i: (i, 0, 0)),
            pl.BlockSpec((CHUNK, cheb, count), lambda i: (first + i, 0, 0)),
            pl.BlockSpec((CHUNK, cheb, count), lambda i: (first + i, 0, 0)),
        ]
        + [pl.BlockSpec(traces[0].shape, lambda i: (0, 0, 0))] * n_sub
        + [pl.BlockSpec(memory_space=pl.ANY)] * has_old,
        out_specs=pl.BlockSpec((cheb, width, LANES), lambda i: (0, first + i, 0)),
        scratch_shapes=[
            pltpu.VMEM((n_sub, 2, 2 * waves, count), F32),
            pltpu.VMEM((n_sub + 1, 2 * waves, count), F32),
        ],
        input_output_aliases={4 + n_sub: 0} if has_old else {},
        compiler_params=params(),
        cost_estimate=pl.CostEstimate(flops=1 << 22, bytes_accessed=4 << 20, transcendentals=0),
        name="finish",
    )(where, particular, lower, upper, *traces, *extra)


def step_order(modes_count):
    return sorted(range(1, modes_count), key=lambda step: (-bin(step >> 1).count("1"), step & 1, step))


def chunked(n_sub, modes_count, fields, previous, eigen_vectors, eigen_map, eigen_magnitude, end_rows):
    cheb, x_local, span_points = fields.shape[1:]
    kz_local, count = previous.shape[1], previous.shape[3]
    stream_points = x_local * modes_count
    chunks = kz_local // CHUNK
    where = jnp.stack([lax.axis_index("modes"), lax.axis_index("sub")]).astype(jnp.int32)
    span_table = jnp.asarray(spanwise_rows(span_points, modes_count, kz_local))
    stream_table = jnp.asarray(streamwise_rows(stream_points, modes_count, count))
    ends = jnp.pad(end_rows[0], ((0, 6), (0, 0)))
    lam = eigen_magnitude.reshape(cheb, 1)
    blocks = count // LANES
    prev = previous.reshape(cheb, kz_local, 2, blocks, LANES).transpose(0, 1, 3, 2, 4)
    prev = prev.reshape(cheb, kz_local * blocks * 2, LANES)

    groups, begin = [], 0
    for share in SHARES:
        size = share * chunks // sum(SHARES)
        groups.append(list(range(begin, begin + size)))
        begin += size

    def joined_exchange(value):
        got = lax.all_to_all(value, "modes", 0, 0, tiled=True)
        return got, [got] * modes_count

    def apart_exchange(values):
        got, flying = [None] * modes_count, []
        got[0] = values[0]
        for step in step_order(modes_count):
            pairs = [(d, d ^ step) for d in range(modes_count)]
            got[step] = lax.ppermute(values[step], "modes", pairs)
            flying.append(got[step])
        return got, flying

    everything = list(range(chunks))
    (head,) = span_part(fields, span_table, where, 0, HEAD_ROWS, [(HEAD_JOINED, everything)], 8)
    sets = list(zip(JOINED, groups))
    bodies = span_part(fields, span_table, where, HEAD_ROWS, cheb - HEAD_ROWS, sets, BODY_BLOCK)
    head, before = (joined_exchange if HEAD_JOINED else apart_exchange)(head)
    lower, upper = wall_shapes(where, cheb, kz_local, count)
    arrived = []
    for at, value in enumerate(bodies):
        if at:
            value, lower, upper, _ = lax.optimization_barrier((value, lower, upper, before[AFTER]))
        value, before = (joined_exchange if JOINED[at] else apart_exchange)(value)
        arrived.append(value)

    out = None
    for group, rest in zip(groups, arrived):
        particular, traces = stream_group(
            where, prev, stream_table, eigen_map[0], eigen_vectors[0], ends, lam,
            group[0], len(group), [head, rest], [group[0], 0], kz_local,
        )
        all_traces = [traces] + [
            lax.ppermute(traces, "sub", [(d, (d + shift) % n_sub) for d in range(n_sub)])
            for shift in range(1, n_sub)
        ]
        out = finish_group(where, particular, lower, upper, all_traces, out, group[0], kz_local)
    out = out.reshape(cheb, kz_local, blocks, 2, LANES).transpose(0, 1, 3, 2, 4)
    return out.reshape(cheb, kz_local, 2, count)


def spanwise_table(wave_index, points):
    grid = jnp.arange(points, dtype=jnp.int32)
    phase = grid[:, None] * wave_index[None, :] % points
    angle = TWO_PI / points * phase.astype(jnp.float32)
    scale = 1.0 / math.sqrt(points)
    return (jnp.stack([jnp.cos(angle), -jnp.sin(angle)], axis=1) * scale).astype(jnp.bfloat16)


def streamwise_table(points, count):
    grid = jnp.arange(points, dtype=jnp.int32)
    waves = jnp.arange(count, dtype=jnp.int32) - count // 2
    phase = grid[:, None] * waves[None, :] % points
    angle = TWO_PI / points * phase.astype(jnp.float32)
    cosine = jnp.cos(angle)
    sine = jnp.sin(angle)
    scale = 1.0 / math.sqrt(points)
    real_row = jnp.concatenate([cosine, -sine], axis=1)
    imag_row = jnp.concatenate([sine, cosine], axis=1)
    return (jnp.stack([real_row, imag_row], axis=1) * scale).astype(jnp.bfloat16)


def wall_terms(kappa, cheb):
    points = jnp.cos(math.pi * (jnp.arange(cheb, dtype=jnp.float32) + 1.0) / (cheb + 1))
    points = points[:, None, None, None]
    rate = kappa[None, :, None, :]
    divisor = 1.0 - jnp.exp(-4.0 * rate)
    lower = (
        jnp.exp(-rate * (1.0 + points)) * (1.0 - jnp.exp(-2.0 * rate * (1.0 - points))) / divisor
    )
    upper = (
        jnp.exp(-rate * (1.0 - points)) * (1.0 - jnp.exp(-2.0 * rate * (1.0 + points))) / divisor
    )
    return (lower, upper)


def plain(fields, previous, eigen_vectors, eigen_map, eigen_magnitude, end_rows):
    high = lax.Precision.HIGHEST
    modes_count = lax.axis_size("modes")
    mode_index = lax.axis_index("modes")
    sub_index = lax.axis_index("sub")
    cheb = fields.shape[1]
    x_local = fields.shape[2]
    span_points = fields.shape[3]
    stream_points = x_local * modes_count
    kz_total = span_points // 4
    kz_local = kz_total // modes_count
    kx_count = previous.shape[3]
    stress = (fields[0].astype(jnp.float32) * fields[1].astype(jnp.float32)).astype(jnp.bfloat16)
    wave_index = jnp.arange(kz_total, dtype=jnp.int32)
    table_z = spanwise_table(wave_index, span_points)
    half_spectrum = jnp.einsum(
        "cxz,zrk->cxrk", stress, table_z, preferred_element_type=jnp.float32
    ).astype(jnp.bfloat16)
    table_x = streamwise_table(stream_points, kx_count)
    kept = lax.all_to_all(half_spectrum, "modes", split_axis=3, concat_axis=1, tiled=True)
    stress_hat = jnp.einsum("cxrk,xrq->ckq", kept, table_x, preferred_element_type=jnp.float32)
    stress_hat = stress_hat.reshape(cheb, kz_local, 2, kx_count)
    waves_x = jnp.arange(kx_count, dtype=jnp.float32) - float(kx_count // 2)
    waves_z = (mode_index * kz_local + jnp.arange(kz_local, dtype=jnp.int32)).astype(jnp.float32)
    kappa_sq = (
        SHIFT_TERM + (WAVE_SCALE * waves_x[None, :]) ** 2 + (WAVE_SCALE * waves_z[:, None]) ** 2
    )
    kappa = jnp.sqrt(kappa_sq)
    decay_four = jnp.exp(-4.0 * kappa)
    coth_term = ((1.0 + decay_four) / (1.0 - decay_four))[:, None, :]
    csch_term = (2.0 * jnp.exp(-2.0 * kappa) / (1.0 - decay_four))[:, None, :]
    freq_x = TWO_PI * waves_x / stream_points
    forcing_re = previous[:, :, 0] + freq_x * stress_hat[:, :, 1]
    forcing_im = previous[:, :, 1] - freq_x * stress_hat[:, :, 0]
    forcing = jnp.stack([forcing_re, forcing_im], axis=2)
    coefficients = jnp.einsum("ij,jkrq->ikrq", eigen_map[0], forcing, precision=high)
    coefficients = coefficients / -(
        eigen_magnitude[:, None, None, None] + kappa_sq[None, :, None, :]
    )
    particular = jnp.einsum("ij,jkrq->ikrq", eigen_vectors[0], coefficients, precision=high)
    traces = jnp.einsum("ej,jkrq->ekrq", end_rows[0], particular, precision=high)
    kappa_wide = kappa[:, None, :]
    gathered = lax.all_gather(traces[None], "sub", axis=0, tiled=True)
    jumps = (gathered[1:, 0] - gathered[:-1, 1]) / kappa_wide
    off_term = -csch_term
    diag_term = 2.0 * coth_term

    def forward(carried, jump_value):
        c_prev, d_prev = carried
        divisor = diag_term - off_term * c_prev
        c_next = off_term / divisor
        d_next = (jump_value - off_term * d_prev) / divisor
        return ((c_next, d_next), (c_next, d_next))

    start_state = (
        jnp.zeros((kz_local, 1, kx_count), jnp.float32),
        jnp.zeros((kz_local, 2, kx_count), jnp.float32),
    )
    unused, (c_values, d_values) = lax.scan(forward, start_state, jumps)

    def backward(g_next, factors):
        c_value, d_value = factors
        g_value = d_value - c_value * g_next
        return (g_value, g_value)

    zero_value = jnp.zeros((kz_local, 2, kx_count), jnp.float32)
    unused_last, solved = lax.scan(backward, zero_value, (c_values, d_values), reverse=True)
    padded = jnp.concatenate([zero_value[None], solved, zero_value[None]], axis=0)
    g_lower = lax.dynamic_index_in_dim(padded, sub_index, 0, keepdims=False)
    g_upper = lax.dynamic_index_in_dim(padded, sub_index + 1, 0, keepdims=False)
    lower, upper = wall_terms(kappa, cheb)
    return particular + g_lower[None] * lower + g_upper[None] * upper


def local(n_sub, modes_count, fields, previous, *rest):
    fits = (
        previous.shape[1] % (CHUNK * sum(SHARES)) == 0
        and modes_count & (modes_count - 1) == 0
        and fields.shape[2] == LANES
        and fields.shape[1] % 96 == 0
        and previous.shape[3] % LANES == 0
    )
    if fits:
        return chunked(n_sub, modes_count, fields, previous, *rest)
    return plain(fields, previous, *rest)


def solution(mesh):
    placed = (
        P(None, "sub", "modes", None),
        P("sub", "modes", None, None),
        P("sub", None, None),
        P("sub", None, None),
        P("sub"),
        P("sub", None, None),
    )
    return jax.shard_map(
        functools.partial(local, mesh.shape["sub"], mesh.shape["modes"]),
        mesh=mesh,
        in_specs=placed,
        out_specs=P("sub", "modes", None, None),
        check_vma=False,
    )
```

```python
import functools
import math

import jax
import jax.numpy as jnp
import ml_dtypes
import numpy as np
from jax import lax
from jax.experimental import pallas as pl
from jax.experimental.pallas import tpu as pltpu
from jax.sharding import PartitionSpec as P

TWO_PI = 2.0 * math.pi
WAVE_SCALE = 0.0007
SHIFT_TERM = 0.06
CHUNK = 4
GROUP = 2 * CHUNK
LANES = 128
BF16 = jnp.bfloat16
F32 = jnp.float32
VMEM_LIMIT = 50 * 1024 * 1024
TILE = 256
Y_PARTS = 1
AFTER = 6
SHARES = (2, 2)
JOINED = (False, True)
HEAD_JOINED = True
BODY_BLOCK = 16
HEAD_ROWS = 32
HEAD_BLOCK = 16


def spanwise_rows(points, modes_count, kz_local):
    grid = np.arange(points)
    waves = np.arange(modes_count * kz_local)
    angle = TWO_PI / points * ((grid[None, :] * waves[:, None]) % points)
    both = np.stack([np.cos(angle), -np.sin(angle)], axis=0) / math.sqrt(points)
    both = both.reshape(2, modes_count, kz_local // CHUNK, CHUNK, points)
    both = both.transpose(1, 2, 0, 3, 4).reshape(modes_count, 2 * kz_local, points)
    return both.astype(np.float32).astype(ml_dtypes.bfloat16)


def streamwise_rows(points, modes_count, count):
    grid = np.arange(points)
    waves = np.arange(count) - count // 2
    angle = TWO_PI / points * ((grid[:, None] * waves[None, :]) % points)
    both = np.concatenate([np.cos(angle), np.sin(angle)], axis=1) / math.sqrt(points)
    both = both.reshape(modes_count, points // modes_count, 2 * count)
    return both.astype(np.float32).astype(ml_dtypes.bfloat16)


def split_pair(value):
    high = value.astype(BF16)
    low = (value - high.astype(F32)).astype(BF16)
    return high, low


def paired_map(matrix):
    high, low = split_pair(matrix)
    return jnp.concatenate(
        [jnp.concatenate([high, high], axis=1), jnp.concatenate([low, low], axis=1)], axis=0
    )


def full_spec():
    return pl.BlockSpec(memory_space=pltpu.VMEM)


def scalar_spec():
    return pl.BlockSpec(memory_space=pltpu.SMEM)


def params(limit=VMEM_LIMIT):
    return pltpu.CompilerParams(vmem_limit_bytes=limit)


def span_kernel(modes_count, sets, block, where, fields, table, *rest):
    outs, rows = rest[:-1], rest[-1]
    per_dest = table.shape[1]
    points = table.shape[2]
    me = where[0]

    @pl.when(pl.program_id(0) == 0)
    def _():
        for step in range(modes_count):
            rows[step * per_dest : (step + 1) * per_dest, :] = table[me ^ step]

    x_local = fields.shape[2]
    for pair in range(block // 2):
        stress = fields[0, 2 * pair : 2 * pair + 2] * fields[1, 2 * pair : 2 * pair + 2]
        stress = stress.reshape(2 * x_local, points)
        spectrum = lax.dot_general(
            rows[...], stress, (((1,), (1,)), ((), ())), preferred_element_type=F32
        )
        span = slice(2 * GROUP * pair, 2 * GROUP * (pair + 1))
        for step in range(modes_count):
            at = 0
            for joined, group in sets:
                for place, chunk in enumerate(group):
                    start = step * per_dest + chunk * GROUP
                    piece = spectrum[start : start + GROUP]
                    piece = jnp.concatenate([piece[:, :x_local], piece[:, x_local:]], axis=0)
                    if joined:
                        outs[at][me ^ step, place, span, :] = piece.astype(BF16)
                    else:
                        outs[at + step][place, span, :] = piece.astype(BF16)
                at += 1 if joined else modes_count


def span_part(fields, table, where, first, count, sets, block):
    modes_count, per_dest, points = table.shape
    x_local = fields.shape[2]
    shapes, specs = [], []
    for joined, group in sets:
        if joined:
            head = (modes_count, len(group))
            shapes.append(jax.ShapeDtypeStruct(head + (count * GROUP, x_local), BF16))
            specs.append(pl.BlockSpec(head + (block * GROUP, x_local), lambda i, w: (0, 0, i, 0)))
            continue
        for _ in range(modes_count):
            shapes.append(jax.ShapeDtypeStruct((len(group), count * GROUP, x_local), BF16))
            specs.append(
                pl.BlockSpec((len(group), block * GROUP, x_local), lambda i, w: (0, i, 0))
            )
    outs = pl.pallas_call(
        functools.partial(span_kernel, modes_count, sets, block),
        out_shape=shapes,
        grid_spec=pltpu.PrefetchScalarGridSpec(
            num_scalar_prefetch=1,
            grid=(count // block,),
            in_specs=[
                pl.BlockSpec((2, block, x_local, points), lambda i, w: (0, first // block + i, 0, 0)),
                pl.BlockSpec(table.shape, lambda i, w: (0, 0, 0)),
            ],
            out_specs=specs,
            scratch_shapes=[pltpu.VMEM((modes_count * per_dest, points), BF16)],
        ),
        compiler_params=params(),
        cost_estimate=pl.CostEstimate(
            flops=2 * count * x_local * points * modes_count * per_dest,
            bytes_accessed=count * x_local * points * 5,
            transcendentals=0,
        ),
        name="span",
    )(where, fields, table)
    result, at = [], 0
    for joined, group in sets:
        if joined:
            result.append(outs[at])
            at += 1
        else:
            result.append(outs[at : at + modes_count])
            at += modes_count
    return result


def kappa_rows(first, rows, count, span):
    waves_x = lax.broadcasted_iota(jnp.int32, (rows, count), 1) - count // 2
    waves_z = lax.broadcasted_iota(jnp.int32, (rows, count), 0) // span + first
    scaled_x = WAVE_SCALE * waves_x.astype(F32)
    scaled_z = WAVE_SCALE * waves_z.astype(F32)
    return SHIFT_TERM + scaled_x * scaled_x + scaled_z * scaled_z


def stream_kernel(modes_count, parts, first, size, kz_local, where, prev, table_ref, m_ref, v_ref, e_ref, lam, *rest):
    arrays_in = sum(part[0] for part in parts)
    sources, rest = rest[:arrays_in], rest[arrays_in:]
    particular, traces_out, held, old_rows, tables, done, forcing, sems, own_sems, out_sems = rest
    cheb = m_ref.shape[0]
    x_local = tables.shape[1]
    count = tables.shape[2] // 2
    width = old_rows.shape[2]
    points = modes_count * x_local
    me = where[0]
    blocks = count // LANES

    def copies(place):
        result, at, row = [], 0, 0
        for part, (arrays, offset, rows) in enumerate(parts):
            for d in range(modes_count):
                if arrays == 1:
                    source = sources[at].at[d, offset + place]
                else:
                    source = sources[at + d].at[offset + place]
                target = held.at[place, d, pl.ds(row, rows)]
                result.append(pltpu.make_async_copy(source, target, sems.at[place, part, d]))
            at += arrays
            row += rows
        return result

    def old_copy(place):
        source = prev.at[:, pl.ds((first + place) * width, width)]
        return pltpu.make_async_copy(source, old_rows.at[place], own_sems.at[place])

    def done_copy(wave):
        return pltpu.make_async_copy(done.at[wave], particular.at[wave], out_sems.at[wave])

    table_copy = pltpu.make_async_copy(table_ref, tables, own_sems.at[size])
    table_copy.start()
    for place in range(size):
        for copy in copies(place):
            copy.start()
        old_copy(place).start()

    waves = (lax.broadcasted_iota(jnp.int32, (1, count), 1) - count // 2).astype(F32)
    weight = TWO_PI * waves / points
    row_in = lax.broadcasted_iota(jnp.int32, (GROUP, count), 0)
    signed = jnp.where(row_in < CHUNK, weight, -weight)
    map_pair = paired_map(m_ref[...])
    end_map = jnp.dot(
        e_ref[...], v_ref[...], preferred_element_type=F32, precision=lax.Precision.HIGHEST
    )
    vector_pair = paired_map(jnp.concatenate([v_ref[...], end_map], axis=0))
    magnitude = lam[...]
    extended = cheb + end_map.shape[0]

    for place in range(size):
        for copy in copies(place):
            copy.wait()
        if place == 0:
            table_copy.wait()
        row = 0
        for arrays, _, rows in parts:
            origin = [d if arrays == 1 else me ^ d for d in range(modes_count)]
            base = row

            def transform(step, unused):
                span = pl.ds(pl.multiple_of(base + step * TILE, TILE), TILE)
                left = jnp.concatenate([held[place, d, span, :] for d in range(modes_count)], axis=1)
                cosine, sine = [
                    jnp.dot(
                        left,
                        jnp.concatenate(
                            [tables[d, :, h * count : (h + 1) * count] for d in origin], axis=0
                        ),
                        preferred_element_type=F32,
                    ).reshape(TILE // GROUP, GROUP, count)
                    for h in range(2)
                ]
                cosine = pltpu.roll(cosine, CHUNK, 1)
                total = signed[None] * cosine - weight[None] * sine
                total = total.reshape(TILE, count)
                for b in range(blocks):
                    forcing[b, span, :] = total[:, b * LANES : (b + 1) * LANES]
                return unused

            lax.fori_loop(0, rows // TILE, transform, 0)
            row += rows

        old_copy(place).wait()
        flat = old_rows.at[place].reshape(cheb * width, LANES)
        for k in range(CHUNK):
            wave = (first + place) * CHUNK + k
            sides = []
            for r in range(2):
                for b in range(blocks):
                    new = forcing[b, pl.ds(r * CHUNK + k, cheb, stride=GROUP), :]
                    old = flat[pl.ds((k * blocks + b) * 2 + r, cheb, stride=width), :]
                    sides.append(new + old)
            side = jnp.concatenate(sides, axis=1)
            mapped = jnp.dot(
                map_pair, jnp.concatenate(split_pair(side), axis=0), preferred_element_type=F32
            )
            mapped = mapped[:cheb] + mapped[cheb:]
            kappa_sq = kappa_rows(me * kz_local + wave, 1, count, 1)
            inverse = -1.0 / (magnitude + kappa_sq)
            coefficients = mapped * jnp.concatenate([inverse, inverse], axis=1)
            pair = jnp.concatenate(split_pair(coefficients), axis=0)
            value = jnp.dot(vector_pair, pair, preferred_element_type=F32)
            value = value[:extended] + value[extended:]
            done[place * CHUNK + k] = value[:cheb]
            done_copy(place * CHUNK + k).start()
            for r in range(2):
                for e in range(2):
                    row = 2 * (place * CHUNK + k) + r
                    traces_out[e, row : row + 1, :] = value[
                        cheb + e : cheb + e + 1, r * count : (r + 1) * count
                    ]
    for wave in range(size * CHUNK):
        done_copy(wave).wait()


def stream_group(where, prev, tables, m_map, v_map, ends, lam, first, size, sources, offsets, kz_local):
    modes_count = tables.shape[0]
    cheb = m_map.shape[0]
    count = tables.shape[2] // 2
    x_local = tables.shape[1]
    flat, parts = [], []
    for source, offset in zip(sources, offsets):
        arrays = list(source) if isinstance(source, (list, tuple)) else [source]
        parts.append((len(arrays), offset, arrays[0].shape[-2]))
        flat += arrays
    rows = sum(part[2] for part in parts)
    flops = 2 * size * rows * modes_count * x_local * 2 * count
    return pl.pallas_call(
        functools.partial(stream_kernel, modes_count, parts, first, size, kz_local),
        out_shape=[
            jax.ShapeDtypeStruct((size * CHUNK, cheb, 2 * count), F32),
            jax.ShapeDtypeStruct((2, size * GROUP, count), F32),
        ],
        in_specs=[scalar_spec()]
        + [pl.BlockSpec(memory_space=pl.ANY)] * 2
        + [full_spec()] * 4
        + [pl.BlockSpec(memory_space=pl.ANY)] * len(flat),
        out_specs=[pl.BlockSpec(memory_space=pl.ANY), full_spec()],
        scratch_shapes=[
            pltpu.VMEM((size, modes_count, rows, x_local), BF16),
            pltpu.VMEM((size, cheb, CHUNK * 2 * count // LANES, LANES), F32),
            pltpu.VMEM(tables.shape, BF16),
            pltpu.VMEM((size * CHUNK, cheb, 2 * count), F32),
            pltpu.VMEM((count // LANES, rows, LANES), F32),
            pltpu.SemaphoreType.DMA((size, len(parts), modes_count)),
            pltpu.SemaphoreType.DMA((size + 1,)),
            pltpu.SemaphoreType.DMA((size * CHUNK,)),
        ],
        compiler_params=params(),
        cost_estimate=pl.CostEstimate(flops=2 * flops, bytes_accessed=4 << 20, transcendentals=0),
        name="stream",
    )(where, prev, tables, m_map, v_map, ends, lam, *flat)


def wall_kernel(kz_local, where, lower_out, upper_out):
    cheb, count = lower_out.shape[1:]
    order = lax.broadcasted_iota(jnp.int32, (cheb, 1), 0).astype(F32)
    points = jnp.cos(math.pi * (order + 1.0) / (cheb + 1))
    chunk = pl.program_id(0)
    for k in range(CHUNK):
        kappa = jnp.sqrt(kappa_rows(where[0] * kz_local + chunk * CHUNK + k, 1, count, 1))
        inverse = 1.0 / (1.0 - jnp.exp(-4.0 * kappa))
        fall = jnp.exp(-kappa * (1.0 + points))
        rise = jnp.exp(-kappa * (1.0 - points))
        lower_out[k] = fall * (1.0 - rise * rise) * inverse
        upper_out[k] = rise * (1.0 - fall * fall) * inverse


def wall_shapes(where, cheb, kz_local, count):
    shape = jax.ShapeDtypeStruct((kz_local, cheb, count), F32)
    return pl.pallas_call(
        functools.partial(wall_kernel, kz_local),
        out_shape=[shape, shape],
        grid=(kz_local // CHUNK,),
        in_specs=[scalar_spec()],
        out_specs=[pl.BlockSpec((CHUNK, cheb, count), lambda i: (i, 0, 0))] * 2,
        compiler_params=params(),
        cost_estimate=pl.CostEstimate(flops=1 << 24, bytes_accessed=6 << 20, transcendentals=2 << 20),
        name="wall",
    )(where)


def finish_kernel(first, kz_local, n_sub, has_old, where, particular, lower, upper, *rest):
    traces = rest[:n_sub]
    out, ordered, solved = rest[n_sub + has_old :]
    held = particular.shape[1]
    count = lower.shape[2]
    rows = traces[0].shape[1]
    me = where[1]

    @pl.when((pl.program_id(0) == 0) & (pl.program_id(1) == 0))
    def _():
        for shift in range(n_sub):
            owner = lax.rem(me + n_sub - shift, n_sub)
            ordered[owner] = traces[shift][...]
        kappa = jnp.sqrt(kappa_rows(where[0] * kz_local + first * CHUNK, rows, count, 2))
        decay = jnp.exp(-4.0 * kappa)
        coth_term = (1.0 + decay) / (1.0 - decay)
        csch_term = 2.0 * jnp.exp(-2.0 * kappa) / (1.0 - decay)
        zero = jnp.zeros((rows, count), F32)
        c_prev, d_prev = zero, zero
        factors = []
        for index in range(1, n_sub):
            jump = (ordered[index, 0] - ordered[index - 1, 1]) / kappa
            inverse = 1.0 / (2.0 * coth_term + csch_term * c_prev)
            c_prev = -csch_term * inverse
            d_prev = (jump + csch_term * d_prev) * inverse
            factors.append((c_prev, d_prev))
        solved[0] = zero
        solved[n_sub] = zero
        g_next = zero
        for index in range(n_sub - 1, 0, -1):
            c_value, d_value = factors[index - 1]
            g_next = d_value - c_value * g_next
            solved[index] = g_next

    blocks = count // LANES
    width = CHUNK * 2 * blocks
    flat = out.reshape(held * width, LANES)
    chunk = pl.program_id(0)
    for k in range(CHUNK):
        wave = chunk * CHUNK + k
        for r in range(2):
            row = 2 * wave + r
            g_lower = solved[me, pl.ds(row, 1), :]
            g_upper = solved[me + 1, pl.ds(row, 1), :]
            value = (
                particular[k, :, r * count : (r + 1) * count]
                + g_lower * lower[k]
                + g_upper * upper[k]
            )
            for b in range(blocks):
                start = (k * blocks + b) * 2 + r
                flat[pl.ds(start, held, stride=width), :] = value[:, b * LANES : (b + 1) * LANES]


def finish_group(where, particular, lower, upper, traces, old, first, kz_local):
    n_sub = len(traces)
    waves, cheb = particular.shape[:2]
    count = lower.shape[2]
    width = CHUNK * 2 * count // LANES
    total = (cheb, kz_local * 2 * count // LANES, LANES)
    has_old = 0 if old is None else 1
    extra = [] if old is None else [old]
    return pl.pallas_call(
        functools.partial(finish_kernel, first, kz_local, n_sub, has_old),
        out_shape=jax.ShapeDtypeStruct(total, F32),
        grid=(waves // CHUNK, Y_PARTS),
        in_specs=[
            scalar_spec(),
            pl.BlockSpec((CHUNK, cheb // Y_PARTS, 2 * count), lambda i, j: (i, j, 0)),
            pl.BlockSpec((CHUNK, cheb // Y_PARTS, count), lambda i, j: (first + i, j, 0)),
            pl.BlockSpec((CHUNK, cheb // Y_PARTS, count), lambda i, j: (first + i, j, 0)),
        ]
        + [pl.BlockSpec(traces[0].shape, lambda i, j: (0, 0, 0))] * n_sub
        + [pl.BlockSpec(memory_space=pl.ANY)] * has_old,
        out_specs=pl.BlockSpec((cheb // Y_PARTS, width, LANES), lambda i, j: (j, first + i, 0)),
        scratch_shapes=[
            pltpu.VMEM((n_sub, 2, 2 * waves, count), F32),
            pltpu.VMEM((n_sub + 1, 2 * waves, count), F32),
        ],
        input_output_aliases={4 + n_sub: 0} if has_old else {},
        compiler_params=params(),
        cost_estimate=pl.CostEstimate(flops=1 << 22, bytes_accessed=4 << 20, transcendentals=0),
        name="finish",
    )(where, particular, lower, upper, *traces, *extra)


def step_order(modes_count):
    return sorted(range(1, modes_count), key=lambda step: (-bin(step >> 1).count("1"), step & 1, step))


def chunked(n_sub, modes_count, fields, previous, eigen_vectors, eigen_map, eigen_magnitude, end_rows):
    cheb, x_local, span_points = fields.shape[1:]
    kz_local, count = previous.shape[1], previous.shape[3]
    stream_points = x_local * modes_count
    chunks = kz_local // CHUNK
    where = jnp.stack([lax.axis_index("modes"), lax.axis_index("sub")]).astype(jnp.int32)
    span_table = jnp.asarray(spanwise_rows(span_points, modes_count, kz_local))
    stream_table = jnp.asarray(streamwise_rows(stream_points, modes_count, count))
    ends = jnp.pad(end_rows[0], ((0, 6), (0, 0)))
    lam = eigen_magnitude.reshape(cheb, 1)
    blocks = count // LANES
    prev = previous.reshape(cheb, kz_local, 2, blocks, LANES).transpose(0, 1, 3, 2, 4)
    prev = prev.reshape(cheb, kz_local * blocks * 2, LANES)

    groups, begin = [], 0
    for share in SHARES:
        size = share * chunks // sum(SHARES)
        groups.append(list(range(begin, begin + size)))
        begin += size

    def joined_exchange(value):
        got = lax.all_to_all(value, "modes", 0, 0, tiled=True)
        return got, [got] * modes_count

    def apart_exchange(values):
        got, flying = [None] * modes_count, []
        got[0] = values[0]
        for step in step_order(modes_count):
            pairs = [(d, d ^ step) for d in range(modes_count)]
            got[step] = lax.ppermute(values[step], "modes", pairs)
            flying.append(got[step])
        return got, flying

    everything = list(range(chunks))
    (head,) = span_part(fields, span_table, where, 0, HEAD_ROWS, [(HEAD_JOINED, everything)], HEAD_BLOCK)
    sets = list(zip(JOINED, groups))
    bodies = span_part(fields, span_table, where, HEAD_ROWS, cheb - HEAD_ROWS, sets, BODY_BLOCK)
    head, before = (joined_exchange if HEAD_JOINED else apart_exchange)(head)
    lower, upper = wall_shapes(where, cheb, kz_local, count)
    arrived = []
    for at, value in enumerate(bodies):
        if at:
            value, lower, upper, _ = lax.optimization_barrier((value, lower, upper, before[:AFTER]))
        value, before = (joined_exchange if JOINED[at] else apart_exchange)(value)
        arrived.append(value)

    out = None
    for group, rest in zip(groups, arrived):
        particular, traces = stream_group(
            where, prev, stream_table, eigen_map[0], eigen_vectors[0], ends, lam,
            group[0], len(group), [head, rest], [group[0], 0], kz_local,
        )
        all_traces = [traces] + [
            lax.ppermute(traces, "sub", [(d, (d + shift) % n_sub) for d in range(n_sub)])
            for shift in range(1, n_sub)
        ]
        out = finish_group(where, particular, lower, upper, all_traces, out, group[0], kz_local)
    out = out.reshape(cheb, kz_local, blocks, 2, LANES).transpose(0, 1, 3, 2, 4)
    return out.reshape(cheb, kz_local, 2, count)


def spanwise_table(wave_index, points):
    grid = jnp.arange(points, dtype=jnp.int32)
    phase = grid[:, None] * wave_index[None, :] % points
    angle = TWO_PI / points * phase.astype(jnp.float32)
    scale = 1.0 / math.sqrt(points)
    return (jnp.stack([jnp.cos(angle), -jnp.sin(angle)], axis=1) * scale).astype(jnp.bfloat16)


def streamwise_table(points, count):
    grid = jnp.arange(points, dtype=jnp.int32)
    waves = jnp.arange(count, dtype=jnp.int32) - count // 2
    phase = grid[:, None] * waves[None, :] % points
    angle = TWO_PI / points * phase.astype(jnp.float32)
    cosine = jnp.cos(angle)
    sine = jnp.sin(angle)
    scale = 1.0 / math.sqrt(points)
    real_row = jnp.concatenate([cosine, -sine], axis=1)
    imag_row = jnp.concatenate([sine, cosine], axis=1)
    return (jnp.stack([real_row, imag_row], axis=1) * scale).astype(jnp.bfloat16)


def wall_terms(kappa, cheb):
    points = jnp.cos(math.pi * (jnp.arange(cheb, dtype=jnp.float32) + 1.0) / (cheb + 1))
    points = points[:, None, None, None]
    rate = kappa[None, :, None, :]
    divisor = 1.0 - jnp.exp(-4.0 * rate)
    lower = (
        jnp.exp(-rate * (1.0 + points)) * (1.0 - jnp.exp(-2.0 * rate * (1.0 - points))) / divisor
    )
    upper = (
        jnp.exp(-rate * (1.0 - points)) * (1.0 - jnp.exp(-2.0 * rate * (1.0 + points))) / divisor
    )
    return (lower, upper)


def plain(fields, previous, eigen_vectors, eigen_map, eigen_magnitude, end_rows):
    high = lax.Precision.HIGHEST
    modes_count = lax.axis_size("modes")
    mode_index = lax.axis_index("modes")
    sub_index = lax.axis_index("sub")
    cheb = fields.shape[1]
    x_local = fields.shape[2]
    span_points = fields.shape[3]
    stream_points = x_local * modes_count
    kz_total = span_points // 4
    kz_local = kz_total // modes_count
    kx_count = previous.shape[3]
    stress = (fields[0].astype(jnp.float32) * fields[1].astype(jnp.float32)).astype(jnp.bfloat16)
    wave_index = jnp.arange(kz_total, dtype=jnp.int32)
    table_z = spanwise_table(wave_index, span_points)
    half_spectrum = jnp.einsum(
        "cxz,zrk->cxrk", stress, table_z, preferred_element_type=jnp.float32
    ).astype(jnp.bfloat16)
    table_x = streamwise_table(stream_points, kx_count)
    kept = lax.all_to_all(half_spectrum, "modes", split_axis=3, concat_axis=1, tiled=True)
    stress_hat = jnp.einsum("cxrk,xrq->ckq", kept, table_x, preferred_element_type=jnp.float32)
    stress_hat = stress_hat.reshape(cheb, kz_local, 2, kx_count)
    waves_x = jnp.arange(kx_count, dtype=jnp.float32) - float(kx_count // 2)
    waves_z = (mode_index * kz_local + jnp.arange(kz_local, dtype=jnp.int32)).astype(jnp.float32)
    kappa_sq = (
        SHIFT_TERM + (WAVE_SCALE * waves_x[None, :]) ** 2 + (WAVE_SCALE * waves_z[:, None]) ** 2
    )
    kappa = jnp.sqrt(kappa_sq)
    decay_four = jnp.exp(-4.0 * kappa)
    coth_term = ((1.0 + decay_four) / (1.0 - decay_four))[:, None, :]
    csch_term = (2.0 * jnp.exp(-2.0 * kappa) / (1.0 - decay_four))[:, None, :]
    freq_x = TWO_PI * waves_x / stream_points
    forcing_re = previous[:, :, 0] + freq_x * stress_hat[:, :, 1]
    forcing_im = previous[:, :, 1] - freq_x * stress_hat[:, :, 0]
    forcing = jnp.stack([forcing_re, forcing_im], axis=2)
    coefficients = jnp.einsum("ij,jkrq->ikrq", eigen_map[0], forcing, precision=high)
    coefficients = coefficients / -(
        eigen_magnitude[:, None, None, None] + kappa_sq[None, :, None, :]
    )
    particular = jnp.einsum("ij,jkrq->ikrq", eigen_vectors[0], coefficients, precision=high)
    traces = jnp.einsum("ej,jkrq->ekrq", end_rows[0], particular, precision=high)
    kappa_wide = kappa[:, None, :]
    gathered = lax.all_gather(traces[None], "sub", axis=0, tiled=True)
    jumps = (gathered[1:, 0] - gathered[:-1, 1]) / kappa_wide
    off_term = -csch_term
    diag_term = 2.0 * coth_term

    def forward(carried, jump_value):
        c_prev, d_prev = carried
        divisor = diag_term - off_term * c_prev
        c_next = off_term / divisor
        d_next = (jump_value - off_term * d_prev) / divisor
        return ((c_next, d_next), (c_next, d_next))

    start_state = (
        jnp.zeros((kz_local, 1, kx_count), jnp.float32),
        jnp.zeros((kz_local, 2, kx_count), jnp.float32),
    )
    unused, (c_values, d_values) = lax.scan(forward, start_state, jumps)

    def backward(g_next, factors):
        c_value, d_value = factors
        g_value = d_value - c_value * g_next
        return (g_value, g_value)

    zero_value = jnp.zeros((kz_local, 2, kx_count), jnp.float32)
    unused_last, solved = lax.scan(backward, zero_value, (c_values, d_values), reverse=True)
    padded = jnp.concatenate([zero_value[None], solved, zero_value[None]], axis=0)
    g_lower = lax.dynamic_index_in_dim(padded, sub_index, 0, keepdims=False)
    g_upper = lax.dynamic_index_in_dim(padded, sub_index + 1, 0, keepdims=False)
    lower, upper = wall_terms(kappa, cheb)
    return particular + g_lower[None] * lower + g_upper[None] * upper


def local(n_sub, modes_count, fields, previous, *rest):
    fits = (
        previous.shape[1] % (CHUNK * sum(SHARES)) == 0
        and modes_count & (modes_count - 1) == 0
        and fields.shape[2] == LANES
        and fields.shape[1] % 96 == 0
        and previous.shape[3] % LANES == 0
    )
    if fits:
        return chunked(n_sub, modes_count, fields, previous, *rest)
    return plain(fields, previous, *rest)


def solution(mesh):
    placed = (
        P(None, "sub", "modes", None),
        P("sub", "modes", None, None),
        P("sub", None, None),
        P("sub", None, None),
        P("sub"),
        P("sub", None, None),
    )
    return jax.shard_map(
        functools.partial(local, mesh.shape["sub"], mesh.shape["modes"]),
        mesh=mesh,
        in_specs=placed,
        out_specs=P("sub", "modes", None, None),
        check_vma=False,
    )
```

```python
import functools
import math

import jax
import jax.numpy as jnp
import ml_dtypes
import numpy as np
from jax import lax
from jax.experimental import pallas as pl
from jax.experimental.pallas import tpu as pltpu
from jax.sharding import PartitionSpec as P

TWO_PI = 2.0 * math.pi
WAVE_SCALE = 0.0007
SHIFT_TERM = 0.06
CHUNK = 4
GROUP = 2 * CHUNK
LANES = 128
BF16 = jnp.bfloat16
F32 = jnp.float32
VMEM_LIMIT = 50 * 1024 * 1024
TILE = 256
Y_PARTS = 1
AFTER = 6
SHARES = (2, 2)
JOINED = (False, True)
HEAD_JOINED = True
BODY_BLOCK = 16
HEAD_ROWS = 32
HEAD_BLOCK = 16


def spanwise_rows(points, modes_count, kz_local):
    grid = np.arange(points)
    waves = np.arange(modes_count * kz_local)
    angle = TWO_PI / points * ((grid[None, :] * waves[:, None]) % points)
    both = np.stack([np.cos(angle), -np.sin(angle)], axis=0) / math.sqrt(points)
    both = both.reshape(2, modes_count, kz_local // CHUNK, CHUNK, points)
    both = both.transpose(1, 2, 0, 3, 4).reshape(modes_count, 2 * kz_local, points)
    return both.astype(np.float32).astype(ml_dtypes.bfloat16)


def streamwise_rows(points, modes_count, count):
    grid = np.arange(points)
    waves = np.arange(count) - count // 2
    angle = TWO_PI / points * ((grid[:, None] * waves[None, :]) % points)
    both = np.concatenate([np.cos(angle), np.sin(angle)], axis=1) / math.sqrt(points)
    both = both.reshape(modes_count, points // modes_count, 2 * count)
    return both.astype(np.float32).astype(ml_dtypes.bfloat16)


def split_pair(value):
    high = value.astype(BF16)
    low = (value - high.astype(F32)).astype(BF16)
    return high, low


def paired_map(matrix):
    high, low = split_pair(matrix)
    return jnp.concatenate(
        [jnp.concatenate([high, high], axis=1), jnp.concatenate([low, low], axis=1)], axis=0
    )


def full_spec():
    return pl.BlockSpec(memory_space=pltpu.VMEM)


def scalar_spec():
    return pl.BlockSpec(memory_space=pltpu.SMEM)


def params(limit=VMEM_LIMIT):
    return pltpu.CompilerParams(vmem_limit_bytes=limit)


def span_kernel(modes_count, sets, block, where, fields, table, *rest):
    outs, rows = rest[:-1], rest[-1]
    per_dest = table.shape[1]
    points = table.shape[2]
    me = where[0]

    @pl.when(pl.program_id(0) == 0)
    def _():
        for step in range(modes_count):
            rows[step * per_dest : (step + 1) * per_dest, :] = table[me ^ step]

    x_local = fields.shape[2]
    for pair in range(block // 2):
        stress = fields[0, 2 * pair : 2 * pair + 2] * fields[1, 2 * pair : 2 * pair + 2]
        stress = stress.reshape(2 * x_local, points)
        spectrum = lax.dot_general(
            rows[...], stress, (((1,), (1,)), ((), ())), preferred_element_type=F32
        )
        span = slice(2 * GROUP * pair, 2 * GROUP * (pair + 1))
        for step in range(modes_count):
            at = 0
            for joined, group in sets:
                for place, chunk in enumerate(group):
                    start = step * per_dest + chunk * GROUP
                    piece = spectrum[start : start + GROUP]
                    piece = jnp.concatenate([piece[:, :x_local], piece[:, x_local:]], axis=0)
                    if joined:
                        outs[at][me ^ step, place, span, :] = piece.astype(BF16)
                    else:
                        outs[at + step][place, span, :] = piece.astype(BF16)
                at += 1 if joined else modes_count


def span_part(fields, table, where, first, count, sets, block):
    modes_count, per_dest, points = table.shape
    x_local = fields.shape[2]
    shapes, specs = [], []
    for joined, group in sets:
        if joined:
            head = (modes_count, len(group))
            shapes.append(jax.ShapeDtypeStruct(head + (count * GROUP, x_local), BF16))
            specs.append(pl.BlockSpec(head + (block * GROUP, x_local), lambda i, w: (0, 0, i, 0)))
            continue
        for _ in range(modes_count):
            shapes.append(jax.ShapeDtypeStruct((len(group), count * GROUP, x_local), BF16))
            specs.append(
                pl.BlockSpec((len(group), block * GROUP, x_local), lambda i, w: (0, i, 0))
            )
    outs = pl.pallas_call(
        functools.partial(span_kernel, modes_count, sets, block),
        out_shape=shapes,
        grid_spec=pltpu.PrefetchScalarGridSpec(
            num_scalar_prefetch=1,
            grid=(count // block,),
            in_specs=[
                pl.BlockSpec((2, block, x_local, points), lambda i, w: (0, first // block + i, 0, 0)),
                pl.BlockSpec(table.shape, lambda i, w: (0, 0, 0)),
            ],
            out_specs=specs,
            scratch_shapes=[pltpu.VMEM((modes_count * per_dest, points), BF16)],
        ),
        compiler_params=params(),
        cost_estimate=pl.CostEstimate(
            flops=2 * count * x_local * points * modes_count * per_dest,
            bytes_accessed=count * x_local * points * 5,
            transcendentals=0,
        ),
        name="span",
    )(where, fields, table)
    result, at = [], 0
    for joined, group in sets:
        if joined:
            result.append(outs[at])
            at += 1
        else:
            result.append(outs[at : at + modes_count])
            at += modes_count
    return result


def kappa_rows(first, rows, count, span):
    waves_x = lax.broadcasted_iota(jnp.int32, (rows, count), 1) - count // 2
    waves_z = lax.broadcasted_iota(jnp.int32, (rows, count), 0) // span + first
    scaled_x = WAVE_SCALE * waves_x.astype(F32)
    scaled_z = WAVE_SCALE * waves_z.astype(F32)
    return SHIFT_TERM + scaled_x * scaled_x + scaled_z * scaled_z


def stream_kernel(modes_count, parts, first, size, kz_local, where, prev, table_ref, m_ref, v_ref, e_ref, lam, *rest):
    arrays_in = sum(part[0] for part in parts)
    sources, rest = rest[:arrays_in], rest[arrays_in:]
    particular, traces_out, held, old_rows, tables, done, forcing, sems, own_sems, out_sems = rest
    cheb = m_ref.shape[0]
    x_local = tables.shape[1]
    count = tables.shape[2] // 2
    width = old_rows.shape[2]
    points = modes_count * x_local
    me = where[0]
    blocks = count // LANES

    def copies(place):
        result, at, row = [], 0, 0
        for part, (arrays, offset, rows) in enumerate(parts):
            for d in range(modes_count):
                if arrays == 1:
                    source = sources[at].at[d, offset + place]
                else:
                    source = sources[at + d].at[offset + place]
                target = held.at[place, d, pl.ds(row, rows)]
                result.append(pltpu.make_async_copy(source, target, sems.at[place, part, d]))
            at += arrays
            row += rows
        return result

    def old_copy(place):
        source = prev.at[:, pl.ds((first + place) * width, width)]
        return pltpu.make_async_copy(source, old_rows.at[place], own_sems.at[place])

    def done_copy(wave):
        return pltpu.make_async_copy(done.at[wave], particular.at[wave], out_sems.at[wave])

    table_copy = pltpu.make_async_copy(table_ref, tables, own_sems.at[size])
    table_copy.start()
    for place in range(size):
        for copy in copies(place):
            copy.start()
        old_copy(place).start()

    waves = (lax.broadcasted_iota(jnp.int32, (1, count), 1) - count // 2).astype(F32)
    weight = TWO_PI * waves / points
    row_in = lax.broadcasted_iota(jnp.int32, (GROUP, count), 0)
    signed = jnp.where(row_in < CHUNK, weight, -weight)
    map_pair = paired_map(m_ref[...])
    end_map = jnp.dot(
        e_ref[...], v_ref[...], preferred_element_type=F32, precision=lax.Precision.HIGHEST
    )
    vector_pair = paired_map(jnp.concatenate([v_ref[...], end_map], axis=0))
    magnitude = lam[...]
    extended = cheb + end_map.shape[0]

    for place in range(size):
        if place == 0:
            table_copy.wait()
        landing = copies(place)
        row = 0
        for part, (arrays, _, rows) in enumerate(parts):
            for copy in landing[part * modes_count : (part + 1) * modes_count]:
                copy.wait()
            origin = [d if arrays == 1 else me ^ d for d in range(modes_count)]
            base = row

            def transform(step, unused):
                span = pl.ds(pl.multiple_of(base + step * TILE, TILE), TILE)
                left = jnp.concatenate([held[place, d, span, :] for d in range(modes_count)], axis=1)
                cosine, sine = [
                    jnp.dot(
                        left,
                        jnp.concatenate(
                            [tables[d, :, h * count : (h + 1) * count] for d in origin], axis=0
                        ),
                        preferred_element_type=F32,
                    ).reshape(TILE // GROUP, GROUP, count)
                    for h in range(2)
                ]
                cosine = pltpu.roll(cosine, CHUNK, 1)
                total = signed[None] * cosine - weight[None] * sine
                total = total.reshape(TILE, count)
                for b in range(blocks):
                    forcing[b, span, :] = total[:, b * LANES : (b + 1) * LANES]
                return unused

            lax.fori_loop(0, rows // TILE, transform, 0)
            row += rows

        old_copy(place).wait()
        flat = old_rows.at[place].reshape(cheb * width, LANES)
        for k in range(CHUNK):
            wave = (first + place) * CHUNK + k
            sides = []
            for r in range(2):
                for b in range(blocks):
                    new = forcing[b, pl.ds(r * CHUNK + k, cheb, stride=GROUP), :]
                    old = flat[pl.ds((k * blocks + b) * 2 + r, cheb, stride=width), :]
                    sides.append(new + old)
            side = jnp.concatenate(sides, axis=1)
            mapped = jnp.dot(
                map_pair, jnp.concatenate(split_pair(side), axis=0), preferred_element_type=F32
            )
            mapped = mapped[:cheb] + mapped[cheb:]
            kappa_sq = kappa_rows(me * kz_local + wave, 1, count, 1)
            inverse = -1.0 / (magnitude + kappa_sq)
            coefficients = mapped * jnp.concatenate([inverse, inverse], axis=1)
            pair = jnp.concatenate(split_pair(coefficients), axis=0)
            value = jnp.dot(vector_pair, pair, preferred_element_type=F32)
            value = value[:extended] + value[extended:]
            done[place * CHUNK + k] = value[:cheb]
            done_copy(place * CHUNK + k).start()
            for r in range(2):
                for e in range(2):
                    row = 2 * (place * CHUNK + k) + r
                    traces_out[e, row : row + 1, :] = value[
                        cheb + e : cheb + e + 1, r * count : (r + 1) * count
                    ]
    for wave in range(size * CHUNK):
        done_copy(wave).wait()


def stream_group(where, prev, tables, m_map, v_map, ends, lam, first, size, sources, offsets, kz_local):
    modes_count = tables.shape[0]
    cheb = m_map.shape[0]
    count = tables.shape[2] // 2
    x_local = tables.shape[1]
    flat, parts = [], []
    for source, offset in zip(sources, offsets):
        arrays = list(source) if isinstance(source, (list, tuple)) else [source]
        parts.append((len(arrays), offset, arrays[0].shape[-2]))
        flat += arrays
    rows = sum(part[2] for part in parts)
    flops = 2 * size * rows * modes_count * x_local * 2 * count
    return pl.pallas_call(
        functools.partial(stream_kernel, modes_count, parts, first, size, kz_local),
        out_shape=[
            jax.ShapeDtypeStruct((size * CHUNK, cheb, 2 * count), F32),
            jax.ShapeDtypeStruct((2, size * GROUP, count), F32),
        ],
        in_specs=[scalar_spec()]
        + [pl.BlockSpec(memory_space=pl.ANY)] * 2
        + [full_spec()] * 4
        + [pl.BlockSpec(memory_space=pl.ANY)] * len(flat),
        out_specs=[pl.BlockSpec(memory_space=pl.ANY), full_spec()],
        scratch_shapes=[
            pltpu.VMEM((size, modes_count, rows, x_local), BF16),
            pltpu.VMEM((size, cheb, CHUNK * 2 * count // LANES, LANES), F32),
            pltpu.VMEM(tables.shape, BF16),
            pltpu.VMEM((size * CHUNK, cheb, 2 * count), F32),
            pltpu.VMEM((count // LANES, rows, LANES), F32),
            pltpu.SemaphoreType.DMA((size, len(parts), modes_count)),
            pltpu.SemaphoreType.DMA((size + 1,)),
            pltpu.SemaphoreType.DMA((size * CHUNK,)),
        ],
        compiler_params=params(),
        cost_estimate=pl.CostEstimate(flops=2 * flops, bytes_accessed=4 << 20, transcendentals=0),
        name="stream",
    )(where, prev, tables, m_map, v_map, ends, lam, *flat)


def wall_kernel(kz_local, where, lower_out, upper_out):
    cheb, count = lower_out.shape[1:]
    order = lax.broadcasted_iota(jnp.int32, (cheb, 1), 0).astype(F32)
    points = jnp.cos(math.pi * (order + 1.0) / (cheb + 1))
    chunk = pl.program_id(0)
    for k in range(CHUNK):
        kappa = jnp.sqrt(kappa_rows(where[0] * kz_local + chunk * CHUNK + k, 1, count, 1))
        inverse = 1.0 / (1.0 - jnp.exp(-4.0 * kappa))
        fall = jnp.exp(-kappa * (1.0 + points))
        rise = jnp.exp(-kappa * (1.0 - points))
        lower_out[k] = fall * (1.0 - rise * rise) * inverse
        upper_out[k] = rise * (1.0 - fall * fall) * inverse


def wall_shapes(where, cheb, kz_local, count):
    shape = jax.ShapeDtypeStruct((kz_local, cheb, count), F32)
    return pl.pallas_call(
        functools.partial(wall_kernel, kz_local),
        out_shape=[shape, shape],
        grid=(kz_local // CHUNK,),
        in_specs=[scalar_spec()],
        out_specs=[pl.BlockSpec((CHUNK, cheb, count), lambda i: (i, 0, 0))] * 2,
        compiler_params=params(58 * 1024 * 1024),
        cost_estimate=pl.CostEstimate(flops=1 << 24, bytes_accessed=6 << 20, transcendentals=2 << 20),
        name="wall",
    )(where)


def finish_kernel(first, kz_local, n_sub, has_old, where, particular, lower, upper, *rest):
    traces = rest[:n_sub]
    out, ordered, solved = rest[n_sub + has_old :]
    held = particular.shape[1]
    count = lower.shape[2]
    rows = traces[0].shape[1]
    me = where[1]

    @pl.when((pl.program_id(0) == 0) & (pl.program_id(1) == 0))
    def _():
        for shift in range(n_sub):
            owner = lax.rem(me + n_sub - shift, n_sub)
            ordered[owner] = traces[shift][...]
        kappa = jnp.sqrt(kappa_rows(where[0] * kz_local + first * CHUNK, rows, count, 2))
        decay = jnp.exp(-4.0 * kappa)
        coth_term = (1.0 + decay) / (1.0 - decay)
        csch_term = 2.0 * jnp.exp(-2.0 * kappa) / (1.0 - decay)
        zero = jnp.zeros((rows, count), F32)
        c_prev, d_prev = zero, zero
        factors = []
        for index in range(1, n_sub):
            jump = (ordered[index, 0] - ordered[index - 1, 1]) / kappa
            inverse = 1.0 / (2.0 * coth_term + csch_term * c_prev)
            c_prev = -csch_term * inverse
            d_prev = (jump + csch_term * d_prev) * inverse
            factors.append((c_prev, d_prev))
        solved[0] = zero
        solved[n_sub] = zero
        g_next = zero
        for index in range(n_sub - 1, 0, -1):
            c_value, d_value = factors[index - 1]
            g_next = d_value - c_value * g_next
            solved[index] = g_next

    blocks = count // LANES
    width = CHUNK * 2 * blocks
    flat = out.reshape(held * width, LANES)
    chunk = pl.program_id(0)
    for k in range(CHUNK):
        wave = chunk * CHUNK + k
        for r in range(2):
            row = 2 * wave + r
            g_lower = solved[me, pl.ds(row, 1), :]
            g_upper = solved[me + 1, pl.ds(row, 1), :]
            value = (
                particular[k, :, r * count : (r + 1) * count]
                + g_lower * lower[k]
                + g_upper * upper[k]
            )
            for b in range(blocks):
                start = (k * blocks + b) * 2 + r
                flat[pl.ds(start, held, stride=width), :] = value[:, b * LANES : (b + 1) * LANES]


def finish_group(where, particular, lower, upper, traces, old, first, kz_local):
    n_sub = len(traces)
    waves, cheb = particular.shape[:2]
    count = lower.shape[2]
    width = CHUNK * 2 * count // LANES
    total = (cheb, kz_local * 2 * count // LANES, LANES)
    has_old = 0 if old is None else 1
    extra = [] if old is None else [old]
    return pl.pallas_call(
        functools.partial(finish_kernel, first, kz_local, n_sub, has_old),
        out_shape=jax.ShapeDtypeStruct(total, F32),
        grid=(waves // CHUNK, Y_PARTS),
        in_specs=[
            scalar_spec(),
            pl.BlockSpec((CHUNK, cheb // Y_PARTS, 2 * count), lambda i, j: (i, j, 0)),
            pl.BlockSpec((CHUNK, cheb // Y_PARTS, count), lambda i, j: (first + i, j, 0)),
            pl.BlockSpec((CHUNK, cheb // Y_PARTS, count), lambda i, j: (first + i, j, 0)),
        ]
        + [pl.BlockSpec(traces[0].shape, lambda i, j: (0, 0, 0))] * n_sub
        + [pl.BlockSpec(memory_space=pl.ANY)] * has_old,
        out_specs=pl.BlockSpec((cheb // Y_PARTS, width, LANES), lambda i, j: (j, first + i, 0)),
        scratch_shapes=[
            pltpu.VMEM((n_sub, 2, 2 * waves, count), F32),
            pltpu.VMEM((n_sub + 1, 2 * waves, count), F32),
        ],
        input_output_aliases={4 + n_sub: 0} if has_old else {},
        compiler_params=params(),
        cost_estimate=pl.CostEstimate(flops=1 << 22, bytes_accessed=4 << 20, transcendentals=0),
        name="finish",
    )(where, particular, lower, upper, *traces, *extra)


def step_order(modes_count):
    return sorted(range(1, modes_count), key=lambda step: (-bin(step >> 1).count("1"), step & 1, step))


def chunked(n_sub, modes_count, fields, previous, eigen_vectors, eigen_map, eigen_magnitude, end_rows):
    cheb, x_local, span_points = fields.shape[1:]
    kz_local, count = previous.shape[1], previous.shape[3]
    stream_points = x_local * modes_count
    chunks = kz_local // CHUNK
    where = jnp.stack([lax.axis_index("modes"), lax.axis_index("sub")]).astype(jnp.int32)
    span_table = jnp.asarray(spanwise_rows(span_points, modes_count, kz_local))
    stream_table = jnp.asarray(streamwise_rows(stream_points, modes_count, count))
    ends = jnp.pad(end_rows[0], ((0, 6), (0, 0)))
    lam = eigen_magnitude.reshape(cheb, 1)
    blocks = count // LANES
    prev = previous.reshape(cheb, kz_local, 2, blocks, LANES).transpose(0, 1, 3, 2, 4)
    prev = prev.reshape(cheb, kz_local * blocks * 2, LANES)

    groups, begin = [], 0
    for share in SHARES:
        size = share * chunks // sum(SHARES)
        groups.append(list(range(begin, begin + size)))
        begin += size

    def joined_exchange(value):
        got = lax.all_to_all(value, "modes", 0, 0, tiled=True)
        return got, [got] * modes_count

    def apart_exchange(values):
        got, flying = [None] * modes_count, []
        got[0] = values[0]
        for step in step_order(modes_count):
            pairs = [(d, d ^ step) for d in range(modes_count)]
            got[step] = lax.ppermute(values[step], "modes", pairs)
            flying.append(got[step])
        return got, flying

    everything = list(range(chunks))
    (head,) = span_part(fields, span_table, where, 0, HEAD_ROWS, [(HEAD_JOINED, everything)], HEAD_BLOCK)
    sets = list(zip(JOINED, groups))
    bodies = span_part(fields, span_table, where, HEAD_ROWS, cheb - HEAD_ROWS, sets, BODY_BLOCK)
    head, before = (joined_exchange if HEAD_JOINED else apart_exchange)(head)
    lower, upper = wall_shapes(where, cheb, kz_local, count)
    arrived = []
    for at, value in enumerate(bodies):
        if at:
            value, lower, upper, _ = lax.optimization_barrier((value, lower, upper, before[:AFTER]))
        value, before = (joined_exchange if JOINED[at] else apart_exchange)(value)
        arrived.append(value)

    out = None
    for group, rest in zip(groups, arrived):
        particular, traces = stream_group(
            where, prev, stream_table, eigen_map[0], eigen_vectors[0], ends, lam,
            group[0], len(group), [head, rest], [group[0], 0], kz_local,
        )
        all_traces = [traces] + [
            lax.ppermute(traces, "sub", [(d, (d + shift) % n_sub) for d in range(n_sub)])
            for shift in range(1, n_sub)
        ]
        out = finish_group(where, particular, lower, upper, all_traces, out, group[0], kz_local)
    out = out.reshape(cheb, kz_local, blocks, 2, LANES).transpose(0, 1, 3, 2, 4)
    return out.reshape(cheb, kz_local, 2, count)


def spanwise_table(wave_index, points):
    grid = jnp.arange(points, dtype=jnp.int32)
    phase = grid[:, None] * wave_index[None, :] % points
    angle = TWO_PI / points * phase.astype(jnp.float32)
    scale = 1.0 / math.sqrt(points)
    return (jnp.stack([jnp.cos(angle), -jnp.sin(angle)], axis=1) * scale).astype(jnp.bfloat16)


def streamwise_table(points, count):
    grid = jnp.arange(points, dtype=jnp.int32)
    waves = jnp.arange(count, dtype=jnp.int32) - count // 2
    phase = grid[:, None] * waves[None, :] % points
    angle = TWO_PI / points * phase.astype(jnp.float32)
    cosine = jnp.cos(angle)
    sine = jnp.sin(angle)
    scale = 1.0 / math.sqrt(points)
    real_row = jnp.concatenate([cosine, -sine], axis=1)
    imag_row = jnp.concatenate([sine, cosine], axis=1)
    return (jnp.stack([real_row, imag_row], axis=1) * scale).astype(jnp.bfloat16)


def wall_terms(kappa, cheb):
    points = jnp.cos(math.pi * (jnp.arange(cheb, dtype=jnp.float32) + 1.0) / (cheb + 1))
    points = points[:, None, None, None]
    rate = kappa[None, :, None, :]
    divisor = 1.0 - jnp.exp(-4.0 * rate)
    lower = (
        jnp.exp(-rate * (1.0 + points)) * (1.0 - jnp.exp(-2.0 * rate * (1.0 - points))) / divisor
    )
    upper = (
        jnp.exp(-rate * (1.0 - points)) * (1.0 - jnp.exp(-2.0 * rate * (1.0 + points))) / divisor
    )
    return (lower, upper)


def plain(fields, previous, eigen_vectors, eigen_map, eigen_magnitude, end_rows):
    high = lax.Precision.HIGHEST
    modes_count = lax.axis_size("modes")
    mode_index = lax.axis_index("modes")
    sub_index = lax.axis_index("sub")
    cheb = fields.shape[1]
    x_local = fields.shape[2]
    span_points = fields.shape[3]
    stream_points = x_local * modes_count
    kz_total = span_points // 4
    kz_local = kz_total // modes_count
    kx_count = previous.shape[3]
    stress = (fields[0].astype(jnp.float32) * fields[1].astype(jnp.float32)).astype(jnp.bfloat16)
    wave_index = jnp.arange(kz_total, dtype=jnp.int32)
    table_z = spanwise_table(wave_index, span_points)
    half_spectrum = jnp.einsum(
        "cxz,zrk->cxrk", stress, table_z, preferred_element_type=jnp.float32
    ).astype(jnp.bfloat16)
    table_x = streamwise_table(stream_points, kx_count)
    kept = lax.all_to_all(half_spectrum, "modes", split_axis=3, concat_axis=1, tiled=True)
    stress_hat = jnp.einsum("cxrk,xrq->ckq", kept, table_x, preferred_element_type=jnp.float32)
    stress_hat = stress_hat.reshape(cheb, kz_local, 2, kx_count)
    waves_x = jnp.arange(kx_count, dtype=jnp.float32) - float(kx_count // 2)
    waves_z = (mode_index * kz_local + jnp.arange(kz_local, dtype=jnp.int32)).astype(jnp.float32)
    kappa_sq = (
        SHIFT_TERM + (WAVE_SCALE * waves_x[None, :]) ** 2 + (WAVE_SCALE * waves_z[:, None]) ** 2
    )
    kappa = jnp.sqrt(kappa_sq)
    decay_four = jnp.exp(-4.0 * kappa)
    coth_term = ((1.0 + decay_four) / (1.0 - decay_four))[:, None, :]
    csch_term = (2.0 * jnp.exp(-2.0 * kappa) / (1.0 - decay_four))[:, None, :]
    freq_x = TWO_PI * waves_x / stream_points
    forcing_re = previous[:, :, 0] + freq_x * stress_hat[:, :, 1]
    forcing_im = previous[:, :, 1] - freq_x * stress_hat[:, :, 0]
    forcing = jnp.stack([forcing_re, forcing_im], axis=2)
    coefficients = jnp.einsum("ij,jkrq->ikrq", eigen_map[0], forcing, precision=high)
    coefficients = coefficients / -(
        eigen_magnitude[:, None, None, None] + kappa_sq[None, :, None, :]
    )
    particular = jnp.einsum("ij,jkrq->ikrq", eigen_vectors[0], coefficients, precision=high)
    traces = jnp.einsum("ej,jkrq->ekrq", end_rows[0], particular, precision=high)
    kappa_wide = kappa[:, None, :]
    gathered = lax.all_gather(traces[None], "sub", axis=0, tiled=True)
    jumps = (gathered[1:, 0] - gathered[:-1, 1]) / kappa_wide
    off_term = -csch_term
    diag_term = 2.0 * coth_term

    def forward(carried, jump_value):
        c_prev, d_prev = carried
        divisor = diag_term - off_term * c_prev
        c_next = off_term / divisor
        d_next = (jump_value - off_term * d_prev) / divisor
        return ((c_next, d_next), (c_next, d_next))

    start_state = (
        jnp.zeros((kz_local, 1, kx_count), jnp.float32),
        jnp.zeros((kz_local, 2, kx_count), jnp.float32),
    )
    unused, (c_values, d_values) = lax.scan(forward, start_state, jumps)

    def backward(g_next, factors):
        c_value, d_value = factors
        g_value = d_value - c_value * g_next
        return (g_value, g_value)

    zero_value = jnp.zeros((kz_local, 2, kx_count), jnp.float32)
    unused_last, solved = lax.scan(backward, zero_value, (c_values, d_values), reverse=True)
    padded = jnp.concatenate([zero_value[None], solved, zero_value[None]], axis=0)
    g_lower = lax.dynamic_index_in_dim(padded, sub_index, 0, keepdims=False)
    g_upper = lax.dynamic_index_in_dim(padded, sub_index + 1, 0, keepdims=False)
    lower, upper = wall_terms(kappa, cheb)
    return particular + g_lower[None] * lower + g_upper[None] * upper


def local(n_sub, modes_count, fields, previous, *rest):
    fits = (
        previous.shape[1] % (CHUNK * sum(SHARES)) == 0
        and modes_count & (modes_count - 1) == 0
        and fields.shape[2] == LANES
        and fields.shape[1] % 96 == 0
        and previous.shape[3] % LANES == 0
    )
    if fits:
        return chunked(n_sub, modes_count, fields, previous, *rest)
    return plain(fields, previous, *rest)


def solution(mesh):
    placed = (
        P(None, "sub", "modes", None),
        P("sub", "modes", None, None),
        P("sub", None, None),
        P("sub", None, None),
        P("sub"),
        P("sub", None, None),
    )
    return jax.shard_map(
        functools.partial(local, mesh.shape["sub"], mesh.shape["modes"]),
        mesh=mesh,
        in_specs=placed,
        out_specs=P("sub", "modes", None, None),
        check_vma=False,
    )
```

```python
import functools
import math

import jax
import jax.numpy as jnp
import ml_dtypes
import numpy as np
from jax import lax
from jax.experimental import pallas as pl
from jax.experimental.pallas import tpu as pltpu
from jax.sharding import PartitionSpec as P

TWO_PI = 2.0 * math.pi
WAVE_SCALE = 0.0007
SHIFT_TERM = 0.06
CHUNK = 4
GROUP = 2 * CHUNK
LANES = 128
BF16 = jnp.bfloat16
F32 = jnp.float32
VMEM_LIMIT = 50 * 1024 * 1024
TILE = 256
Y_PARTS = 1
AFTER = 6
SHARES = (2, 2)
JOINED = (False, True)
HEAD_JOINED = True
BODY_BLOCK = 16
HEAD_ROWS = 32
HEAD_BLOCK = 16


def spanwise_rows(points, modes_count, kz_local):
    grid = np.arange(points)
    waves = np.arange(modes_count * kz_local)
    angle = TWO_PI / points * ((grid[None, :] * waves[:, None]) % points)
    both = np.stack([np.cos(angle), -np.sin(angle)], axis=0) / math.sqrt(points)
    both = both.reshape(2, modes_count, kz_local // CHUNK, CHUNK, points)
    both = both.transpose(1, 2, 0, 3, 4).reshape(modes_count, 2 * kz_local, points)
    return both.astype(np.float32).astype(ml_dtypes.bfloat16)


def streamwise_rows(points, modes_count, count):
    grid = np.arange(points)
    waves = np.arange(count) - count // 2
    angle = TWO_PI / points * ((grid[:, None] * waves[None, :]) % points)
    both = np.concatenate([np.cos(angle), np.sin(angle)], axis=1) / math.sqrt(points)
    both = both.reshape(modes_count, points // modes_count, 2 * count)
    return both.astype(np.float32).astype(ml_dtypes.bfloat16)


def split_pair(value):
    high = value.astype(BF16)
    low = (value - high.astype(F32)).astype(BF16)
    return high, low


def paired_map(matrix):
    high, low = split_pair(matrix)
    return jnp.concatenate(
        [jnp.concatenate([high, high], axis=1), jnp.concatenate([low, low], axis=1)], axis=0
    )


def full_spec():
    return pl.BlockSpec(memory_space=pltpu.VMEM)


def scalar_spec():
    return pl.BlockSpec(memory_space=pltpu.SMEM)


def params(limit=VMEM_LIMIT):
    return pltpu.CompilerParams(vmem_limit_bytes=limit)


def span_kernel(modes_count, sets, block, where, fields, table, *rest):
    outs, rows = rest[:-1], rest[-1]
    per_dest = table.shape[1]
    points = table.shape[2]
    me = where[0]

    @pl.when(pl.program_id(0) == 0)
    def _():
        for step in range(modes_count):
            rows[step * per_dest : (step + 1) * per_dest, :] = table[me ^ step]

    x_local = fields.shape[2]
    for pair in range(block // 2):
        stress = fields[0, 2 * pair : 2 * pair + 2] * fields[1, 2 * pair : 2 * pair + 2]
        stress = stress.reshape(2 * x_local, points)
        spectrum = lax.dot_general(
            rows[...], stress, (((1,), (1,)), ((), ())), preferred_element_type=F32
        )
        span = slice(2 * GROUP * pair, 2 * GROUP * (pair + 1))
        for step in range(modes_count):
            at = 0
            for joined, group in sets:
                for place, chunk in enumerate(group):
                    start = step * per_dest + chunk * GROUP
                    piece = spectrum[start : start + GROUP]
                    piece = jnp.concatenate([piece[:, :x_local], piece[:, x_local:]], axis=0)
                    if joined:
                        outs[at][me ^ step, place, span, :] = piece.astype(BF16)
                    else:
                        outs[at + step][place, span, :] = piece.astype(BF16)
                at += 1 if joined else modes_count


def span_part(fields, table, where, first, count, sets, block):
    modes_count, per_dest, points = table.shape
    x_local = fields.shape[2]
    shapes, specs = [], []
    for joined, group in sets:
        if joined:
            head = (modes_count, len(group))
            shapes.append(jax.ShapeDtypeStruct(head + (count * GROUP, x_local), BF16))
            specs.append(pl.BlockSpec(head + (block * GROUP, x_local), lambda i, w: (0, 0, i, 0)))
            continue
        for _ in range(modes_count):
            shapes.append(jax.ShapeDtypeStruct((len(group), count * GROUP, x_local), BF16))
            specs.append(
                pl.BlockSpec((len(group), block * GROUP, x_local), lambda i, w: (0, i, 0))
            )
    outs = pl.pallas_call(
        functools.partial(span_kernel, modes_count, sets, block),
        out_shape=shapes,
        grid_spec=pltpu.PrefetchScalarGridSpec(
            num_scalar_prefetch=1,
            grid=(count // block,),
            in_specs=[
                pl.BlockSpec((2, block, x_local, points), lambda i, w: (0, first // block + i, 0, 0)),
                pl.BlockSpec(table.shape, lambda i, w: (0, 0, 0)),
            ],
            out_specs=specs,
            scratch_shapes=[pltpu.VMEM((modes_count * per_dest, points), BF16)],
        ),
        compiler_params=params(),
        cost_estimate=pl.CostEstimate(
            flops=2 * count * x_local * points * modes_count * per_dest,
            bytes_accessed=count * x_local * points * 5,
            transcendentals=0,
        ),
        name="span",
    )(where, fields, table)
    result, at = [], 0
    for joined, group in sets:
        if joined:
            result.append(outs[at])
            at += 1
        else:
            result.append(outs[at : at + modes_count])
            at += modes_count
    return result


def kappa_rows(first, rows, count, span):
    waves_x = lax.broadcasted_iota(jnp.int32, (rows, count), 1) - count // 2
    waves_z = lax.broadcasted_iota(jnp.int32, (rows, count), 0) // span + first
    scaled_x = WAVE_SCALE * waves_x.astype(F32)
    scaled_z = WAVE_SCALE * waves_z.astype(F32)
    return SHIFT_TERM + scaled_x * scaled_x + scaled_z * scaled_z


def stream_kernel(modes_count, parts, first, size, kz_local, where, prev, table_ref, m_ref, v_ref, e_ref, lam, *rest):
    arrays_in = sum(part[0] for part in parts)
    sources, rest = rest[:arrays_in], rest[arrays_in:]
    particular, traces_out, held, old_rows, tables, done, forcing, sems, own_sems, out_sems = rest
    cheb = m_ref.shape[0]
    x_local = tables.shape[1]
    count = tables.shape[2] // 2
    width = old_rows.shape[2]
    points = modes_count * x_local
    me = where[0]
    blocks = count // LANES

    def copies(place):
        result, at, row = [], 0, 0
        for part, (arrays, offset, rows) in enumerate(parts):
            for d in range(modes_count):
                if arrays == 1:
                    source = sources[at].at[d, offset + place]
                else:
                    source = sources[at + d].at[offset + place]
                target = held.at[place, d, pl.ds(row, rows)]
                result.append(pltpu.make_async_copy(source, target, sems.at[place, part, d]))
            at += arrays
            row += rows
        return result

    def old_copy(place):
        source = prev.at[:, pl.ds((first + place) * width, width)]
        return pltpu.make_async_copy(source, old_rows.at[place], own_sems.at[place])

    def done_copy(wave):
        return pltpu.make_async_copy(done.at[wave], particular.at[wave], out_sems.at[wave])

    table_copy = pltpu.make_async_copy(table_ref, tables, own_sems.at[size])
    table_copy.start()
    for place in range(size):
        for copy in copies(place):
            copy.start()
        old_copy(place).start()

    waves = (lax.broadcasted_iota(jnp.int32, (1, count), 1) - count // 2).astype(F32)
    weight = TWO_PI * waves / points
    row_in = lax.broadcasted_iota(jnp.int32, (GROUP, count), 0)
    signed = jnp.where(row_in < CHUNK, weight, -weight)
    map_pair = paired_map(m_ref[...])
    end_map = jnp.dot(
        e_ref[...], v_ref[...], preferred_element_type=F32, precision=lax.Precision.HIGHEST
    )
    vector_pair = paired_map(jnp.concatenate([v_ref[...], end_map], axis=0))
    magnitude = lam[...]
    extended = cheb + end_map.shape[0]

    for place in range(size):
        if place == 0:
            table_copy.wait()
        landing = copies(place)
        row = 0
        for part, (arrays, _, rows) in enumerate(parts):
            for copy in landing[part * modes_count : (part + 1) * modes_count]:
                copy.wait()
            origin = [d if arrays == 1 else me ^ d for d in range(modes_count)]
            base = row

            def transform(step, unused):
                span = pl.ds(pl.multiple_of(base + step * TILE, TILE), TILE)
                left = jnp.concatenate([held[place, d, span, :] for d in range(modes_count)], axis=1)
                cosine, sine = [
                    jnp.dot(
                        left,
                        jnp.concatenate(
                            [tables[d, :, h * count : (h + 1) * count] for d in origin], axis=0
                        ),
                        preferred_element_type=F32,
                    ).reshape(TILE // GROUP, GROUP, count)
                    for h in range(2)
                ]
                cosine = pltpu.roll(cosine, CHUNK, 1)
                total = signed[None] * cosine - weight[None] * sine
                total = total.reshape(TILE, count)
                for b in range(blocks):
                    forcing[b, span, :] = total[:, b * LANES : (b + 1) * LANES]
                return unused

            lax.fori_loop(0, rows // TILE, transform, 0)
            row += rows

        old_copy(place).wait()
        flat = old_rows.at[place].reshape(cheb * width, LANES)
        for k in range(CHUNK):
            wave = (first + place) * CHUNK + k
            sides = []
            for r in range(2):
                for b in range(blocks):
                    new = forcing[b, pl.ds(r * CHUNK + k, cheb, stride=GROUP), :]
                    old = flat[pl.ds((k * blocks + b) * 2 + r, cheb, stride=width), :]
                    sides.append(new + old)
            side = jnp.concatenate(sides, axis=1)
            mapped = jnp.dot(
                map_pair, jnp.concatenate(split_pair(side), axis=0), preferred_element_type=F32
            )
            mapped = mapped[:cheb] + mapped[cheb:]
            kappa_sq = kappa_rows(me * kz_local + wave, 1, count, 1)
            inverse = -1.0 / (magnitude + kappa_sq)
            coefficients = mapped * jnp.concatenate([inverse, inverse], axis=1)
            pair = jnp.concatenate(split_pair(coefficients), axis=0)
            value = jnp.dot(vector_pair, pair, preferred_element_type=F32)
            value = value[:extended] + value[extended:]
            done[place * CHUNK + k] = value[:cheb]
            done_copy(place * CHUNK + k).start()
            for r in range(2):
                for e in range(2):
                    row = 2 * (place * CHUNK + k) + r
                    traces_out[e, row : row + 1, :] = value[
                        cheb + e : cheb + e + 1, r * count : (r + 1) * count
                    ]
    for wave in range(size * CHUNK):
        done_copy(wave).wait()


def stream_group(where, prev, tables, m_map, v_map, ends, lam, first, size, sources, offsets, kz_local):
    modes_count = tables.shape[0]
    cheb = m_map.shape[0]
    count = tables.shape[2] // 2
    x_local = tables.shape[1]
    flat, parts = [], []
    for source, offset in zip(sources, offsets):
        arrays = list(source) if isinstance(source, (list, tuple)) else [source]
        parts.append((len(arrays), offset, arrays[0].shape[-2]))
        flat += arrays
    rows = sum(part[2] for part in parts)
    flops = 2 * size * rows * modes_count * x_local * 2 * count
    return pl.pallas_call(
        functools.partial(stream_kernel, modes_count, parts, first, size, kz_local),
        out_shape=[
            jax.ShapeDtypeStruct((size * CHUNK, cheb, 2 * count), F32),
            jax.ShapeDtypeStruct((2, size * GROUP, count), F32),
        ],
        in_specs=[scalar_spec()]
        + [pl.BlockSpec(memory_space=pl.ANY)] * 2
        + [full_spec()] * 4
        + [pl.BlockSpec(memory_space=pl.ANY)] * len(flat),
        out_specs=[pl.BlockSpec(memory_space=pl.ANY), full_spec()],
        scratch_shapes=[
            pltpu.VMEM((size, modes_count, rows, x_local), BF16),
            pltpu.VMEM((size, cheb, CHUNK * 2 * count // LANES, LANES), F32),
            pltpu.VMEM(tables.shape, BF16),
            pltpu.VMEM((size * CHUNK, cheb, 2 * count), F32),
            pltpu.VMEM((count // LANES, rows, LANES), F32),
            pltpu.SemaphoreType.DMA((size, len(parts), modes_count)),
            pltpu.SemaphoreType.DMA((size + 1,)),
            pltpu.SemaphoreType.DMA((size * CHUNK,)),
        ],
        compiler_params=params(58 * 1024 * 1024),
        cost_estimate=pl.CostEstimate(flops=2 * flops, bytes_accessed=4 << 20, transcendentals=0),
        name="stream",
    )(where, prev, tables, m_map, v_map, ends, lam, *flat)


def wall_kernel(kz_local, where, lower_out, upper_out):
    cheb, count = lower_out.shape[1:]
    order = lax.broadcasted_iota(jnp.int32, (cheb, 1), 0).astype(F32)
    points = jnp.cos(math.pi * (order + 1.0) / (cheb + 1))
    chunk = pl.program_id(0)
    for k in range(CHUNK):
        kappa = jnp.sqrt(kappa_rows(where[0] * kz_local + chunk * CHUNK + k, 1, count, 1))
        inverse = 1.0 / (1.0 - jnp.exp(-4.0 * kappa))
        fall = jnp.exp(-kappa * (1.0 + points))
        rise = jnp.exp(-kappa * (1.0 - points))
        lower_out[k] = fall * (1.0 - rise * rise) * inverse
        upper_out[k] = rise * (1.0 - fall * fall) * inverse


def wall_shapes(where, cheb, kz_local, count):
    shape = jax.ShapeDtypeStruct((kz_local, cheb, count), F32)
    return pl.pallas_call(
        functools.partial(wall_kernel, kz_local),
        out_shape=[shape, shape],
        grid=(kz_local // CHUNK,),
        in_specs=[scalar_spec()],
        out_specs=[pl.BlockSpec((CHUNK, cheb, count), lambda i: (i, 0, 0))] * 2,
        compiler_params=params(58 * 1024 * 1024),
        cost_estimate=pl.CostEstimate(flops=1 << 24, bytes_accessed=6 << 20, transcendentals=2 << 20),
        name="wall",
    )(where)


def finish_kernel(first, kz_local, n_sub, has_old, where, particular, lower, upper, *rest):
    traces = rest[:n_sub]
    out, ordered, solved = rest[n_sub + has_old :]
    held = particular.shape[1]
    count = lower.shape[2]
    rows = traces[0].shape[1]
    me = where[1]

    @pl.when((pl.program_id(0) == 0) & (pl.program_id(1) == 0))
    def _():
        for shift in range(n_sub):
            owner = lax.rem(me + n_sub - shift, n_sub)
            ordered[owner] = traces[shift][...]
        kappa = jnp.sqrt(kappa_rows(where[0] * kz_local + first * CHUNK, rows, count, 2))
        decay = jnp.exp(-4.0 * kappa)
        coth_term = (1.0 + decay) / (1.0 - decay)
        csch_term = 2.0 * jnp.exp(-2.0 * kappa) / (1.0 - decay)
        zero = jnp.zeros((rows, count), F32)
        c_prev, d_prev = zero, zero
        factors = []
        for index in range(1, n_sub):
            jump = (ordered[index, 0] - ordered[index - 1, 1]) / kappa
            inverse = 1.0 / (2.0 * coth_term + csch_term * c_prev)
            c_prev = -csch_term * inverse
            d_prev = (jump + csch_term * d_prev) * inverse
            factors.append((c_prev, d_prev))
        solved[0] = zero
        solved[n_sub] = zero
        g_next = zero
        for index in range(n_sub - 1, 0, -1):
            c_value, d_value = factors[index - 1]
            g_next = d_value - c_value * g_next
            solved[index] = g_next

    blocks = count // LANES
    width = CHUNK * 2 * blocks
    flat = out.reshape(held * width, LANES)
    chunk = pl.program_id(0)
    for k in range(CHUNK):
        wave = chunk * CHUNK + k
        for r in range(2):
            row = 2 * wave + r
            g_lower = solved[me, pl.ds(row, 1), :]
            g_upper = solved[me + 1, pl.ds(row, 1), :]
            value = (
                particular[k, :, r * count : (r + 1) * count]
                + g_lower * lower[k]
                + g_upper * upper[k]
            )
            for b in range(blocks):
                start = (k * blocks + b) * 2 + r
                flat[pl.ds(start, held, stride=width), :] = value[:, b * LANES : (b + 1) * LANES]


def finish_group(where, particular, lower, upper, traces, old, first, kz_local):
    n_sub = len(traces)
    waves, cheb = particular.shape[:2]
    count = lower.shape[2]
    width = CHUNK * 2 * count // LANES
    total = (cheb, kz_local * 2 * count // LANES, LANES)
    has_old = 0 if old is None else 1
    extra = [] if old is None else [old]
    return pl.pallas_call(
        functools.partial(finish_kernel, first, kz_local, n_sub, has_old),
        out_shape=jax.ShapeDtypeStruct(total, F32),
        grid=(waves // CHUNK, Y_PARTS),
        in_specs=[
            scalar_spec(),
            pl.BlockSpec((CHUNK, cheb // Y_PARTS, 2 * count), lambda i, j: (i, j, 0)),
            pl.BlockSpec((CHUNK, cheb // Y_PARTS, count), lambda i, j: (first + i, j, 0)),
            pl.BlockSpec((CHUNK, cheb // Y_PARTS, count), lambda i, j: (first + i, j, 0)),
        ]
        + [pl.BlockSpec(traces[0].shape, lambda i, j: (0, 0, 0))] * n_sub
        + [pl.BlockSpec(memory_space=pl.ANY)] * has_old,
        out_specs=pl.BlockSpec((cheb // Y_PARTS, width, LANES), lambda i, j: (j, first + i, 0)),
        scratch_shapes=[
            pltpu.VMEM((n_sub, 2, 2 * waves, count), F32),
            pltpu.VMEM((n_sub + 1, 2 * waves, count), F32),
        ],
        input_output_aliases={4 + n_sub: 0} if has_old else {},
        compiler_params=params(),
        cost_estimate=pl.CostEstimate(flops=1 << 22, bytes_accessed=4 << 20, transcendentals=0),
        name="finish",
    )(where, particular, lower, upper, *traces, *extra)


def step_order(modes_count):
    return sorted(range(1, modes_count), key=lambda step: (-bin(step >> 1).count("1"), step & 1, step))


def chunked(n_sub, modes_count, fields, previous, eigen_vectors, eigen_map, eigen_magnitude, end_rows):
    cheb, x_local, span_points = fields.shape[1:]
    kz_local, count = previous.shape[1], previous.shape[3]
    stream_points = x_local * modes_count
    chunks = kz_local // CHUNK
    where = jnp.stack([lax.axis_index("modes"), lax.axis_index("sub")]).astype(jnp.int32)
    span_table = jnp.asarray(spanwise_rows(span_points, modes_count, kz_local))
    stream_table = jnp.asarray(streamwise_rows(stream_points, modes_count, count))
    ends = jnp.pad(end_rows[0], ((0, 6), (0, 0)))
    lam = eigen_magnitude.reshape(cheb, 1)
    blocks = count // LANES
    prev = previous.reshape(cheb, kz_local, 2, blocks, LANES).transpose(0, 1, 3, 2, 4)
    prev = prev.reshape(cheb, kz_local * blocks * 2, LANES)

    groups, begin = [], 0
    for share in SHARES:
        size = share * chunks // sum(SHARES)
        groups.append(list(range(begin, begin + size)))
        begin += size

    def joined_exchange(value):
        got = lax.all_to_all(value, "modes", 0, 0, tiled=True)
        return got, [got] * modes_count

    def apart_exchange(values):
        got, flying = [None] * modes_count, []
        got[0] = values[0]
        for step in step_order(modes_count):
            pairs = [(d, d ^ step) for d in range(modes_count)]
            got[step] = lax.ppermute(values[step], "modes", pairs)
            flying.append(got[step])
        return got, flying

    everything = list(range(chunks))
    (head,) = span_part(fields, span_table, where, 0, HEAD_ROWS, [(HEAD_JOINED, everything)], HEAD_BLOCK)
    sets = list(zip(JOINED, groups))
    bodies = span_part(fields, span_table, where, HEAD_ROWS, cheb - HEAD_ROWS, sets, BODY_BLOCK)
    head, before = (joined_exchange if HEAD_JOINED else apart_exchange)(head)
    lower, upper = wall_shapes(where, cheb, kz_local, count)
    arrived = []
    for at, value in enumerate(bodies):
        if at:
            value, lower, upper, _ = lax.optimization_barrier((value, lower, upper, before[:AFTER]))
        value, before = (joined_exchange if JOINED[at] else apart_exchange)(value)
        arrived.append(value)

    out = None
    for group, rest in zip(groups, arrived):
        particular, traces = stream_group(
            where, prev, stream_table, eigen_map[0], eigen_vectors[0], ends, lam,
            group[0], len(group), [head, rest], [group[0], 0], kz_local,
        )
        all_traces = [traces] + [
            lax.ppermute(traces, "sub", [(d, (d + shift) % n_sub) for d in range(n_sub)])
            for shift in range(1, n_sub)
        ]
        out = finish_group(where, particular, lower, upper, all_traces, out, group[0], kz_local)
    out = out.reshape(cheb, kz_local, blocks, 2, LANES).transpose(0, 1, 3, 2, 4)
    return out.reshape(cheb, kz_local, 2, count)


def spanwise_table(wave_index, points):
    grid = jnp.arange(points, dtype=jnp.int32)
    phase = grid[:, None] * wave_index[None, :] % points
    angle = TWO_PI / points * phase.astype(jnp.float32)
    scale = 1.0 / math.sqrt(points)
    return (jnp.stack([jnp.cos(angle), -jnp.sin(angle)], axis=1) * scale).astype(jnp.bfloat16)


def streamwise_table(points, count):
    grid = jnp.arange(points, dtype=jnp.int32)
    waves = jnp.arange(count, dtype=jnp.int32) - count // 2
    phase = grid[:, None] * waves[None, :] % points
    angle = TWO_PI / points * phase.astype(jnp.float32)
    cosine = jnp.cos(angle)
    sine = jnp.sin(angle)
    scale = 1.0 / math.sqrt(points)
    real_row = jnp.concatenate([cosine, -sine], axis=1)
    imag_row = jnp.concatenate([sine, cosine], axis=1)
    return (jnp.stack([real_row, imag_row], axis=1) * scale).astype(jnp.bfloat16)


def wall_terms(kappa, cheb):
    points = jnp.cos(math.pi * (jnp.arange(cheb, dtype=jnp.float32) + 1.0) / (cheb + 1))
    points = points[:, None, None, None]
    rate = kappa[None, :, None, :]
    divisor = 1.0 - jnp.exp(-4.0 * rate)
    lower = (
        jnp.exp(-rate * (1.0 + points)) * (1.0 - jnp.exp(-2.0 * rate * (1.0 - points))) / divisor
    )
    upper = (
        jnp.exp(-rate * (1.0 - points)) * (1.0 - jnp.exp(-2.0 * rate * (1.0 + points))) / divisor
    )
    return (lower, upper)


def plain(fields, previous, eigen_vectors, eigen_map, eigen_magnitude, end_rows):
    high = lax.Precision.HIGHEST
    modes_count = lax.axis_size("modes")
    mode_index = lax.axis_index("modes")
    sub_index = lax.axis_index("sub")
    cheb = fields.shape[1]
    x_local = fields.shape[2]
    span_points = fields.shape[3]
    stream_points = x_local * modes_count
    kz_total = span_points // 4
    kz_local = kz_total // modes_count
    kx_count = previous.shape[3]
    stress = (fields[0].astype(jnp.float32) * fields[1].astype(jnp.float32)).astype(jnp.bfloat16)
    wave_index = jnp.arange(kz_total, dtype=jnp.int32)
    table_z = spanwise_table(wave_index, span_points)
    half_spectrum = jnp.einsum(
        "cxz,zrk->cxrk", stress, table_z, preferred_element_type=jnp.float32
    ).astype(jnp.bfloat16)
    table_x = streamwise_table(stream_points, kx_count)
    kept = lax.all_to_all(half_spectrum, "modes", split_axis=3, concat_axis=1, tiled=True)
    stress_hat = jnp.einsum("cxrk,xrq->ckq", kept, table_x, preferred_element_type=jnp.float32)
    stress_hat = stress_hat.reshape(cheb, kz_local, 2, kx_count)
    waves_x = jnp.arange(kx_count, dtype=jnp.float32) - float(kx_count // 2)
    waves_z = (mode_index * kz_local + jnp.arange(kz_local, dtype=jnp.int32)).astype(jnp.float32)
    kappa_sq = (
        SHIFT_TERM + (WAVE_SCALE * waves_x[None, :]) ** 2 + (WAVE_SCALE * waves_z[:, None]) ** 2
    )
    kappa = jnp.sqrt(kappa_sq)
    decay_four = jnp.exp(-4.0 * kappa)
    coth_term = ((1.0 + decay_four) / (1.0 - decay_four))[:, None, :]
    csch_term = (2.0 * jnp.exp(-2.0 * kappa) / (1.0 - decay_four))[:, None, :]
    freq_x = TWO_PI * waves_x / stream_points
    forcing_re = previous[:, :, 0] + freq_x * stress_hat[:, :, 1]
    forcing_im = previous[:, :, 1] - freq_x * stress_hat[:, :, 0]
    forcing = jnp.stack([forcing_re, forcing_im], axis=2)
    coefficients = jnp.einsum("ij,jkrq->ikrq", eigen_map[0], forcing, precision=high)
    coefficients = coefficients / -(
        eigen_magnitude[:, None, None, None] + kappa_sq[None, :, None, :]
    )
    particular = jnp.einsum("ij,jkrq->ikrq", eigen_vectors[0], coefficients, precision=high)
    traces = jnp.einsum("ej,jkrq->ekrq", end_rows[0], particular, precision=high)
    kappa_wide = kappa[:, None, :]
    gathered = lax.all_gather(traces[None], "sub", axis=0, tiled=True)
    jumps = (gathered[1:, 0] - gathered[:-1, 1]) / kappa_wide
    off_term = -csch_term
    diag_term = 2.0 * coth_term

    def forward(carried, jump_value):
        c_prev, d_prev = carried
        divisor = diag_term - off_term * c_prev
        c_next = off_term / divisor
        d_next = (jump_value - off_term * d_prev) / divisor
        return ((c_next, d_next), (c_next, d_next))

    start_state = (
        jnp.zeros((kz_local, 1, kx_count), jnp.float32),
        jnp.zeros((kz_local, 2, kx_count), jnp.float32),
    )
    unused, (c_values, d_values) = lax.scan(forward, start_state, jumps)

    def backward(g_next, factors):
        c_value, d_value = factors
        g_value = d_value - c_value * g_next
        return (g_value, g_value)

    zero_value = jnp.zeros((kz_local, 2, kx_count), jnp.float32)
    unused_last, solved = lax.scan(backward, zero_value, (c_values, d_values), reverse=True)
    padded = jnp.concatenate([zero_value[None], solved, zero_value[None]], axis=0)
    g_lower = lax.dynamic_index_in_dim(padded, sub_index, 0, keepdims=False)
    g_upper = lax.dynamic_index_in_dim(padded, sub_index + 1, 0, keepdims=False)
    lower, upper = wall_terms(kappa, cheb)
    return particular + g_lower[None] * lower + g_upper[None] * upper


def local(n_sub, modes_count, fields, previous, *rest):
    fits = (
        previous.shape[1] % (CHUNK * sum(SHARES)) == 0
        and modes_count & (modes_count - 1) == 0
        and fields.shape[2] == LANES
        and fields.shape[1] % 96 == 0
        and previous.shape[3] % LANES == 0
    )
    if fits:
        return chunked(n_sub, modes_count, fields, previous, *rest)
    return plain(fields, previous, *rest)


def solution(mesh):
    placed = (
        P(None, "sub", "modes", None),
        P("sub", "modes", None, None),
        P("sub", None, None),
        P("sub", None, None),
        P("sub"),
        P("sub", None, None),
    )
    return jax.shard_map(
        functools.partial(local, mesh.shape["sub"], mesh.shape["modes"]),
        mesh=mesh,
        in_specs=placed,
        out_specs=P("sub", "modes", None, None),
        check_vma=False,
    )
```
